256 devices in a mesh: dp: 16 (over z, core), expert: 16 (over x, y).
Axes of the slice: x: 4, y: 4, z: 8, core: 2. Of those that a mesh axis runs over, the one named last changes fastest.
Arguments:
- tokens: bfloat16 [16, 1024, 4096], P('dp', 'expert'), may hold values from -6 to 6
- attn_gain: float32 [4096], replicated, may hold values from 0.1 to 1.9
- moe_gain: float32 [4096], replicated, may hold values from 0.1 to 1.9
- w_query: bfloat16 [4096, 4096], P('dp', 'expert'), may hold values from -4 to 4
- w_key: bfloat16 [4096, 256], P('dp'), may hold values from -0.1 to 0.1
- w_value: bfloat16 [4096, 256], P('dp'), may hold values from -0.09375 to 0.09375
- w_out: bfloat16 [4096, 4096], P('expert', 'dp'), may hold values from -0.09375 to 0.09375
- expert_gate: bfloat16 [16, 4096, 768], P('expert', 'dp'), may hold values from -0.09375 to 0.09375
- expert_up: bfloat16 [16, 4096, 768], P('expert', 'dp'), may hold values from -0.09375 to 0.09375
- expert_down: bfloat16 [16, 768, 4096], P('expert', 'dp'), may hold values from -0.21875 to 0.21875
- routes: int32 [16, 1024, 8], P('dp', 'expert'), may hold values from 0 to 15, all different within a row; in each aligned block of 64 rows (0 to 63, 64 to 127, ..., all dimensions but the last counted through in order) at most 48 rows name the same one
- route_weights: float32 [16, 1024, 8], P('dp', 'expert'), may hold values from 0.05 to 1
Outputs:
- layer_out: bfloat16 [16, 1024, 4096], P('dp', 'expert')
The draws below stay inside these ranges and needn't reach their ends.
Inputs may be any that keep to these rules, and one draw needn't show every extreme that they name: `routes`: each token names 8 different experts; among the rows of one device no expert is named by more than 48 tokens, and in every draw some expert is named by exactly 48 tokens of some device.
All inputs are finite; a program needn't handle non-finite values.
Results may differ from the reference program's by a relative error of at most 0.012.
Values may be sent and summed in bfloat16 or wider, within the bound.
A program may use at most 128 MiB of HBM per device.

```python
import math
import jax
import jax.numpy as jnp
import numpy as np
from jax import lax

D = 4096
HEADS = 32
KVH = 2
HD = 128
FF = 768
EXPERTS = 16
TOPK = 8
TOK_DEV = 64
CAP = 48
SEQ = 1024
ROLLOUTS = 16
N_DP = 16
N_EXPERT = 16


def shared_keys(key):
    return jax.random.normal(key, (D, KVH * HD), jnp.float32) * D ** (-0.5)


def draw_w_key(key, part):
    key_base = shared_keys(key)
    return jnp.clip(key_base, -0.099609375, 0.099609375).astype(jnp.bfloat16)


def draw_w_query(key, part):
    key = jax.random.fold_in(key, 7)
    own_part = jax.random.normal(key, (D, HEADS * HD), jnp.float32) * D ** (-0.5)
    return jnp.clip(own_part, -4.0, 4.0).astype(jnp.bfloat16)


def draw_tokens(key, part):
    key = jax.random.fold_in(key, 3)
    return jnp.clip(jax.random.normal(key, (ROLLOUTS, SEQ, D), jnp.float32), -6.0, 6.0).astype(jnp.bfloat16)


def block_levels(stream_key, dims, shards, smallest, largest):
    level = 1.0
    for axis_at, parts in shards:
        heights = jax.random.uniform(jax.random.fold_in(jax.random.fold_in(stream_key, 6), axis_at), (parts,), jnp.float32, smallest / len(shards), largest / len(shards))
        level = level * jnp.repeat(jnp.exp(heights), dims[axis_at] // parts).reshape((-1,) + (1,) * (len(dims) - 1 - axis_at))
    return level


def routed_block(stream_key, own, number, rows, count, top, limit, lean):
    order = jax.random.permutation(stream_key, count)
    heavy_load, ordinary = portions_of(count, rows * top, limit, lean, True), portions_of(count, rows * top, limit, lean, False)
    places = jnp.arange(count)

    def named(sizes, rotation):
        used = int((sizes > 0).sum())
        fixed = max(1, used // 4)
        shifted = fixed + (places - fixed + rotation * (used - fixed)) % max(1, count - fixed)
        return jnp.zeros((count,), jnp.int32).at[order[jnp.where(places < fixed, places, shifted)]].set(jnp.asarray(sizes, jnp.int32))

    sizes = jnp.where(number % 4 == 0, named(heavy_load, number // 4), named(ordinary, number - number // 4 - 1))
    mixed = jax.random.permutation(jax.random.fold_in(own, 3), count)
    source_of, receiver = mixed[0:count // 2 * 2:2], mixed[1:count // 2 * 2:2]
    room = jnp.minimum(sizes[source_of] - 1, limit - sizes[receiver]) // 2
    room = jnp.where((source_of == order[0]) | (receiver == order[0]) | (sizes[receiver] == 0), 0, jnp.maximum(room, 0))
    shifted = jax.random.randint(jax.random.fold_in(own, 4), (count // 2,), 0, 1 << 20) % (room + 1)
    sizes = sizes.at[source_of].add(-shifted).at[receiver].add(shifted)
    members = jnp.searchsorted(jnp.cumsum(sizes), jnp.arange(rows * top), side="right").astype(jnp.int32)
    table = members.reshape(top, rows).T
    table = table[jax.random.permutation(jax.random.fold_in(own, 1), rows)]
    rotation = jax.random.randint(jax.random.fold_in(own, 2), (rows, 1), 0, top)
    return jnp.take_along_axis(table, (jnp.arange(top)[None, :] + rotation) % top, axis=1)


def portions_of(number_of, total, reach, lean, full):
    weights = [(1 << 20) // math.isqrt(standing ** lean) + 1 for standing in range(1, number_of + 1)]
    largest = reach if full else min(reach, max(-(-total // number_of), total * weights[0] // sum(weights)))
    least = 1 if total - largest >= number_of - 1 else 0
    holding, spare = [largest] + [least] * (number_of - 1), total - largest - least * (number_of - 1)
    while spare > 0:
        movable = [i for i in range(1, number_of) if holding[i] < largest] or [i for i in range(1, number_of) if holding[i] < reach]
        pool, budget = sum([weights[i] for i in movable]), spare
        for i in movable:
            more = min(reach - holding[i], max(1, budget * weights[i] // pool), spare)
            holding[i] = holding[i] + more
            spare = spare - more
    return np.array(holding)


def normal_values(stream_key, shape, scale, reach, split=(), kind=jnp.bfloat16):
    result = scale * jax.random.normal(stream_key, shape, jnp.float32)
    if split:
        result = result * block_levels(stream_key, shape, split, -0.22, 0.18)
    return jnp.clip(result, -reach, reach).astype(kind)


def setup_inputs(seed: int = 0) -> dict:
    splits = jax.random.split(jax.random.key(seed), 13)
    tokens = draw_tokens(jax.random.fold_in(splits[12], 71), 0)
    attn_gain = jnp.clip(1.0 + 0.18 * jax.random.normal(splits[1], (D,), jnp.float32), 0.1, 1.9)
    moe_gain = jnp.clip(1.0 + 0.18 * jax.random.normal(splits[2], (D,), jnp.float32), 0.1, 1.9)
    w_query = draw_w_query(jax.random.fold_in(splits[12], 71), 0)
    w_key = draw_w_key(jax.random.fold_in(splits[12], 71), 0)
    w_value = normal_values(splits[5], (D, KVH * HD), D ** -0.5, 0.09375, ((0, 16),))
    w_out = normal_values(splits[6], (HEADS * HD, D), (HEADS * HD) ** -0.5, 0.09375, ((0, 16), (1, 16)))
    expert_gate = normal_values(splits[7], (EXPERTS, D, FF), D ** -0.5, 0.09375, ((0, 16), (1, 16)))
    expert_up = normal_values(splits[8], (EXPERTS, D, FF), D ** -0.5, 0.09375, ((0, 16), (1, 16)))
    expert_down = normal_values(splits[9], (EXPERTS, FF, D), FF ** -0.5, 0.21875, ((0, 16), (1, 16)))
    routes_keys = jax.random.split(jax.random.fold_in(splits[10], 1), ROLLOUTS * SEQ // TOK_DEV)
    routes_turns = jax.random.permutation(jax.random.fold_in(splits[10], 3), ROLLOUTS * SEQ // TOK_DEV)
    routes = jax.vmap(lambda own, number: routed_block(jax.random.fold_in(splits[10], 2), own, number, TOK_DEV, EXPERTS, TOPK, CAP, 2))(routes_keys, routes_turns).reshape((ROLLOUTS, SEQ, TOPK))
    route_weights = jnp.clip(jnp.exp(math.log(1.0) - 2.9957323 * jax.random.uniform(splits[11], (ROLLOUTS, SEQ, TOPK), jnp.float32) ** block_levels(splits[11], (ROLLOUTS, SEQ, TOPK), ((0, 16), (1, 16)), -0.2, 0.2)), 0.05, 1.0)
    return {"tokens": tokens, "attn_gain": attn_gain, "moe_gain": moe_gain, "w_query": w_query, "w_key": w_key, "w_value": w_value, "w_out": w_out, "expert_gate": expert_gate, "expert_up": expert_up, "expert_down": expert_down, "routes": routes, "route_weights": route_weights}


def rms_norm(values, gain):
    values = values.astype(jnp.float32)
    return values * lax.rsqrt(lax.optimization_barrier(jnp.mean(values * values, axis=-1, keepdims=True)) + 1e-06) * gain

def rotate(tensor, positions):
    half_dim = tensor.shape[-1] // 2
    frequency = jnp.exp(jnp.arange(half_dim, dtype=jnp.float32) * (-2.0 * math.log(1000000.0) / tensor.shape[-1]))
    angles = positions[:, None] * frequency[None, :]
    cosine = jnp.cos(angles)[:, None, :]
    sine_table = jnp.sin(angles)[:, None, :]
    lower_half = tensor[..., :half_dim]
    upper_half = tensor[..., half_dim:]
    return jnp.concatenate([lower_half * cosine - upper_half * sine_table, upper_half * cosine + lower_half * sine_table], axis=-1)

def reference(tokens, attn_gain, moe_gain, w_query, w_key, w_value, w_out, expert_gate, expert_up, expert_down, routes, route_weights):
    group_size = HEADS // KVH
    per_dev = HEADS // N_EXPERT
    positions = jnp.arange(SEQ, dtype=jnp.float32)
    causal = jnp.arange(SEQ)[:, None] >= jnp.arange(SEQ)[None, :]

    def one_rollout(rollout_rows):
        normed = rms_norm(rollout_rows, attn_gain).astype(jnp.bfloat16)
        queries = jnp.dot(normed, w_query, preferred_element_type=jnp.float32).reshape(SEQ, HEADS, HD)
        key_rows = jnp.dot(normed, w_key, preferred_element_type=jnp.float32).reshape(SEQ, KVH, HD)
        values = jnp.dot(normed, w_value, preferred_element_type=jnp.float32).astype(jnp.bfloat16)
        queries = rotate(queries, positions).astype(jnp.bfloat16)
        key_rows = rotate(key_rows, positions).astype(jnp.bfloat16)
        key_rows = jnp.repeat(key_rows, group_size, axis=1)
        values = jnp.repeat(values.reshape(SEQ, KVH, HD), group_size, axis=1)
        scores = jnp.einsum('qhd,khd->hqk', queries.astype(jnp.float32), key_rows.astype(jnp.float32)) / math.sqrt(HD)
        scores = jnp.where(causal[None], scores, -1e+30)
        scores = scores - lax.optimization_barrier(jnp.max(scores, axis=-1, keepdims=True))
        exp_scores = jnp.exp(scores)
        probs = (exp_scores / lax.optimization_barrier(jnp.sum(exp_scores, axis=-1, keepdims=True))).astype(jnp.bfloat16)
        mixed_heads = jnp.einsum('hqk,khd->qhd', probs.astype(jnp.float32), values.astype(jnp.float32)).astype(jnp.bfloat16)
        mixed_heads = mixed_heads.reshape(SEQ, N_EXPERT, per_dev * HD)
        out_mats = w_out.reshape(N_EXPERT, per_dev * HD, D)
        partial_value = jnp.einsum('sgc,gcd->gsd', mixed_heads.astype(jnp.float32), out_mats.astype(jnp.float32))
        partial_value = lax.optimization_barrier(partial_value.astype(jnp.bfloat16)).astype(jnp.float32)
        return rollout_rows.astype(jnp.float32) + lax.optimization_barrier(jnp.sum(partial_value, axis=0))
    residual = lax.map(one_rollout, tokens)
    flat_rows = residual.reshape(-1, D)
    moe_in = rms_norm(flat_rows, moe_gain).astype(jnp.bfloat16)
    picked_ids = routes.reshape(-1, TOPK)
    shares = route_weights.reshape(-1, TOPK).astype(jnp.float32)
    shares = shares / lax.optimization_barrier(jnp.sum(shares, axis=-1, keepdims=True))
    max_rows = N_DP * N_EXPERT * CAP

    def one_expert(running, inputs):
        expert_id, gate_mat, up_mat, down_mat = inputs
        matched = picked_ids == expert_id
        share_of = lax.optimization_barrier(jnp.sum(jnp.where(matched, shares, 0.0), axis=1))
        chosen = jnp.any(matched, axis=1)
        picked_rows = jnp.nonzero(chosen, size=max_rows, fill_value=0)[0]
        live_rows = jnp.arange(max_rows) < jnp.sum(chosen.astype(jnp.int32))
        inputs_rows = moe_in[picked_rows]
        gated = jnp.dot(inputs_rows, gate_mat, preferred_element_type=jnp.float32)
        lifted = jnp.dot(inputs_rows, up_mat, preferred_element_type=jnp.float32)
        active = (jax.nn.silu(gated) * lifted).astype(jnp.bfloat16)
        produced = jnp.dot(active, down_mat, preferred_element_type=jnp.float32).astype(jnp.bfloat16)
        weighting = jnp.where(live_rows, share_of[picked_rows], 0.0)
        running = running.at[picked_rows].add(produced.astype(jnp.float32) * weighting[:, None])
        return (running, None)
    expert_mix, _ = lax.scan(one_expert, jnp.zeros(flat_rows.shape, jnp.float32), (jnp.arange(EXPERTS, dtype=jnp.int32), expert_gate, expert_up, expert_down))
    return (flat_rows + expert_mix).astype(jnp.bfloat16).reshape(tokens.shape)
```

```python
import functools
import math

import jax
import jax.numpy as jnp
import numpy as np
from jax import lax
from jax.experimental import pallas as pl
from jax.experimental.pallas import tpu as pltpu
from jax.sharding import PartitionSpec as P

HD = 128
D = 4096
FF = 768
TOK = 64
HALF = 32
SEQ = 1024
EXTRA = 128
MESH = pl.DeviceIdType.MESH
F32 = jnp.float32
BF16 = jnp.bfloat16
MIB = 1 << 20

STEP = (0, 3, 1, 2)


def place():
    index = lax.axis_index("expert")
    x, y = index // 4, index % 4
    return (
        (x, y, lambda first, second: {"expert": first * 4 + second}),
        (y, x, lambda first, second: {"expert": second * 4 + first}),
    )


def turn(coordinate, step):
    return (coordinate + step) % 4


def meet(spots):
    barrier = pltpu.get_barrier_semaphore()
    for first, second, device in spots:
        for step in (1, 3):
            pl.semaphore_signal(
                barrier, inc=1, device_id=device(turn(first, step), second), device_id_type=MESH
            )
    pl.semaphore_wait(barrier, 4)


def remote(source, target, sends, recvs, slot, device):
    copy = pltpu.make_async_remote_copy(
        src_ref=source,
        dst_ref=target,
        send_sem=sends.at[slot],
        recv_sem=recvs.at[slot],
        device_id=device,
        device_id_type=MESH,
    )
    copy.start()
    return copy


class Gather:
    def __init__(self, spots, block, sends, recvs, own, absolute):
        self.spots, self.block, self.sends, self.recvs = spots, block, sends, recvs
        self.own, self.absolute = own, absolute
        self.copies = {}

    def send(self, half, group, lane, source, target, device):
        slot = (half * 5 + group) * 4 + lane
        self.copies[half, group, lane] = remote(
            source, target, self.sends, self.recvs, slot, device
        )

    def first_hop(self):
        for half, (f, s, device) in enumerate(self.spots):
            for lane, step in ((0, 1), (1, 3)):
                target = self.block(0 if self.absolute else 1 + lane, half, s, 0, HALF)
                self.send(half, 4, lane, self.own(half), target, device(turn(f, step), s))
        self.spread(0)

    def spread(self, r, halves=(0, 1)):
        for half in halves:
            f, s, device = self.spots[half]
            mine = self.own(half) if r == 0 else self.block(r, half, s, 0, HALF)
            for lane, step in ((0, 1), (1, 3)):
                self.send(half, r, lane, mine, self.block(r, half, s, 0, HALF), device(f, turn(s, step)))

    def second_hop(self):
        for lane, step in ((0, 1), (1, 3)):
            for half, (f, s, device) in enumerate(self.spots):
                self.copies[half, 4, lane].wait_recv()
                source = self.block(1 + lane, half, s, lane * 16, 16)
                target = source if self.absolute else self.block(3, half, s, lane * 16, 16)
                self.send(half, 4, 2 + lane, source, target, device(turn(f, step), s))
                self.spread(1 + lane, (half,))

    def last_hop(self):
        for half in (0, 1):
            for lane in (2, 3):
                self.copies[half, 4, lane].wait_recv()
            self.spread(3, (half,))

    def forward(self, r):
        for lane, step in ((0, 1), (1, 3)):
            for half, (f, s, device) in enumerate(self.spots):
                self.copies[half, r, lane].wait_recv()
                here = self.block(r, half, turn(s, 4 - step), lane * 16, 16)
                self.send(half, r, 2 + lane, here, here, device(f, turn(s, step)))

    def finish(self, r):
        for half in (0, 1):
            for lane in (2, 3):
                self.copies[half, r, lane].wait_recv()

    def rest(self):
        self.second_hop()
        self.forward(0)
        self.last_hop()
        for r in (1, 2, 3):
            self.forward(r)
        for r in range(4):
            self.finish(r)
        self.drain()

    def drain(self):
        for copy in self.copies.values():
            copy.wait_send()


class Scatter:
    def __init__(self, spots, y_ref, small, large, z_ref, sends, recvs):
        self.spots, self.y, self.small, self.large, self.z = spots, y_ref, small, large, z_ref
        self.sends, self.recvs = sends, recvs
        self.copies = {}

    def send(self, half, group, lane, source, target, device):
        slot = (half * 5 + group) * 4 + lane
        self.copies[half, group, lane] = remote(
            source, target, self.sends, self.recvs, slot, device
        )

    def parts(self, half, group):
        f, s, device = self.spots[half]
        if group < 4:
            return (
                lambda step: self.y.at[group, half, turn(s, step)],
                lambda step: device(f, turn(s, step)),
            )
        return (
            lambda step: self.z.at[half, STEP.index(step)],
            lambda step: device(turn(f, step), s),
        )

    def start(self, group):
        for half in (0, 1):
            block, device = self.parts(half, group)
            for lane, step in ((0, 1), (1, 3)):
                self.send(
                    half, group, lane, block(2).at[pl.ds(lane * 16, 16)], self.small.at[half, group, lane],
                    device(step),
                )

    def middle(self, group):
        for lane, step in ((0, 1), (1, 3)):
            for half in (0, 1):
                block, device = self.parts(half, group)
                self.copies[half, group, lane].wait_recv()
                rows = block(step).at[pl.ds(lane * 16, 16)]
                rows[...] = (rows[...].astype(F32) + self.small[half, group, lane].astype(F32)).astype(BF16)
                self.send(half, group, 2 + lane, block(step), self.large.at[half, group, lane], device(step))

    def arrived(self, half, group):
        for lane in (2, 3):
            self.copies[half, group, lane].wait_recv()
        return self.large[half, group, 0].astype(F32) + self.large[half, group, 1].astype(F32)

    def finish(self, group):
        for half in (0, 1):
            _, s, _ = self.spots[half]
            total = self.arrived(half, group) + self.y[group, half, s].astype(F32)
            self.z[half, group] = total.astype(BF16)

    def total(self, half):
        return self.arrived(half, 4) + self.z[half, 0].astype(F32)

    def drain(self):
        for copy in self.copies.values():
            copy.wait_send()


def normalized(values, gain):
    return values * lax.rsqrt(jnp.mean(values * values, axis=-1, keepdims=True) + 1e-06) * gain


def gather_kernel(
    tokens, gain, routes, weights, gate, up, down,
    out, extra, shard,
    own, sends, recvs, local, packed,
):
    packs = [
        (part.at[:, pl.ds(c * 256, 256)], shard.at[pl.ds(at + c * 256, 256)])
        for part, at in ((gate, 0), (up, FF))
        for c in range(3)
    ]
    packs += [(down.at[:, pl.ds(c * 256, 256)], shard.at[pl.ds(2 * FF + c * 48, 48)]) for c in range(16)]
    packs = [pltpu.make_async_copy(source, target, packed.at[i]) for i, (source, target) in enumerate(packs)]
    for copy in packs:
        copy.start()
    spots = place()
    index = lax.axis_index("expert")
    own[...] = normalized(tokens[...].astype(F32), gain[...]).astype(BF16)
    keep = pltpu.make_async_copy(own, out.at[index], local)
    keep.start()
    meet(spots)

    def block(r, half, second, start, rows):
        f, _, device = spots[half]
        return out.at[device(turn(f, STEP[r]), second)["expert"], pl.ds(half * HALF + start, rows)]

    gather = Gather(spots, block, sends, recvs, lambda half: own.at[pl.ds(half * HALF, HALF)], True)
    gather.first_hop()

    share = weights[...] / jnp.sum(weights[...], axis=-1, keepdims=True)
    high = share.astype(BF16).astype(F32)
    low = share - high
    lanes = lax.broadcasted_iota(jnp.int32, (TOK, EXTRA), 1)
    table = jnp.zeros((TOK, EXTRA), F32)
    for k in range(routes.shape[1]):
        named = routes[:, k : k + 1]
        table += jnp.where(lanes == named, high[:, k : k + 1], 0.0)
        table += jnp.where(lanes == named + 16, low[:, k : k + 1], 0.0)
    extra[...] = table.astype(BF16)

    gather.rest()
    keep.wait()
    for copy in packs:
        copy.wait()


def attend(
    gathered, weights, tokens, cosine, sine, gain, extra,
    residual, everyone,
    x, w, queries, keys, values, mixed, moe_in, y, small, large, z, sends, recvs, out_sends, out_recvs, local,
):
    spots = place()
    load_w = pltpu.make_async_copy(weights, w, local.at[0])
    load_w.start()
    load_x = pltpu.make_async_copy(gathered, x, local.at[1])
    load_x.start()
    meet(spots)
    load_w.wait()
    load_x.wait()

    def rope(part, rows):
        return part * cosine[rows] + pltpu.roll(part, HD // 2, 1) * sine[rows]

    @pl.loop(0, 4)
    def _(i):
        rows = pl.ds(pl.multiple_of(i * 256, 256), 256)
        left = x[pl.ds(i * 4, 4)].reshape(256, D)
        q = jnp.dot(left, w[:, 0:256].reshape(D, 256), preferred_element_type=F32)
        for head in (0, 1):
            queries[head, rows] = rope(q[:, head * HD : (head + 1) * HD], rows).astype(BF16)
        kv = jnp.dot(left, w[:, 256:512].reshape(D, 256), preferred_element_type=F32)
        keys[rows] = rope(kv[:, :HD], rows).astype(BF16)
        values[rows] = kv[:, HD:].astype(BF16)

    for i in range(4):
        many = (i + 1) * 256
        for head in (0, 1):
            scores = lax.dot_general(
                queries[head, i * 256 : many], keys[0:many], (((1,), (1,)), ((), ())), preferred_element_type=F32
            ) * (1.0 / math.sqrt(HD))
            at_row = lax.broadcasted_iota(jnp.int32, (256, many), 0) + i * 256
            at_col = lax.broadcasted_iota(jnp.int32, (256, many), 1)
            scores = jnp.where(at_row >= at_col, scores, -1e30)
            grown = jnp.exp(scores - jnp.max(scores, axis=-1, keepdims=True))
            total = jnp.sum(grown, axis=-1, keepdims=True)
            part = jnp.dot(grown.astype(BF16), values[0:many], preferred_element_type=F32) / total
            mixed[i * 4 : i * 4 + 4, :, head * HD : (head + 1) * HD] = part.astype(BF16).reshape(4, TOK, HD)

    scatter = Scatter(spots, y, small, large, z, sends, recvs)

    def project(r):
        picked = []
        for half, (f, s, device) in enumerate(spots):
            for second in range(4):
                at = device(turn(f, STEP[r]), second)["expert"]
                picked.append(mixed[at, half * HALF : (half + 1) * HALF])
        left = jnp.concatenate(picked, axis=0)

        @pl.loop(0, 16)
        def _(d):
            part = jnp.dot(left, w[d, 512:768], preferred_element_type=F32)
            cols = pl.ds(pl.multiple_of(d * 256, 256), 256)
            y[r, :, :, :, cols] = part.astype(BF16).reshape(2, 4, HALF, 256)

    for r in (3, 2, 1, 0):
        project(r)
        scatter.start(r)
    for r in (3, 2, 1):
        scatter.middle(r)
    scatter.finish(3)
    scatter.start(4)
    scatter.middle(0)
    scatter.finish(2)
    scatter.finish(1)
    scatter.middle(4)
    scatter.finish(0)
    for half in (0, 1):
        rows = slice(half * HALF, (half + 1) * HALF)
        summed = tokens[rows].astype(F32) + scatter.total(half)
        residual[rows] = summed
        moe_in[rows, 0:D] = normalized(summed, gain[...]).astype(BF16)
    moe_in[:, D:] = extra[...]

    def block(r, half, second, start, rows):
        return everyone.at[r, half, second, pl.ds(start, rows)]

    gather = Gather(spots, block, out_sends, out_recvs, lambda half: moe_in.at[pl.ds(half * HALF, HALF)], False)
    gather.first_hop()
    keeps = []
    for half, (_, s, _) in enumerate(spots):
        keeps.append(pltpu.make_async_copy(gather.own(half), block(0, half, s, 0, HALF), local.at[half]))
        keeps[-1].start()
    scatter.drain()
    gather.rest()
    for keep in keeps:
        keep.wait()


def experts(
    everyone, weights, residual,
    out,
    g, w, act, y, small, large, z, sends, recvs, load_g, load_w, load_down,
):
    spots = place()
    rows_of = [pltpu.make_async_copy(everyone.at[r], g.at[r], load_g.at[r]) for r in range(4)]
    feeds = []
    for c in range(6):
        part = (c // 2 + c % 2 * 3) * 256
        view = pl.ds(part, 256)
        feeds.append(pltpu.make_async_copy(weights.at[:, view], w.at[:, view], load_w.at[c]))
    view = pl.ds(2 * FF, FF)
    downs = pltpu.make_async_copy(weights.at[:, view], w.at[:, view], load_down)
    rows_of[3].start()
    for copy in feeds:
        copy.start()
    for r in (2, 1, 0):
        rows_of[r].start()
    downs.start()
    meet(spots)
    scatter = Scatter(spots, y, small, large, z, sends, recvs)
    index = lax.axis_index("expert")

    def feed_part(r, c):
        cols = pl.ds(c * 256, 256)
        left = g[r, :, :, :, 0:D].reshape(256, D)
        gate = jnp.dot(left, w[:, cols].reshape(D, 256), preferred_element_type=F32)
        up = jnp.dot(left, w[:, pl.ds(FF + c * 256, 256)].reshape(D, 256), preferred_element_type=F32)
        act[:, cols] = (gate / (1.0 + jnp.exp(-gate)) * up).astype(BF16)

    def feed(r):
        rows_of[r].wait()
        for c in range(3):
            if r == 3:
                feeds[2 * c].wait()
                feeds[2 * c + 1].wait()
            feed_part(r, c)

    def down(r):
        table = g[r, :, :, :, D:].reshape(256, EXTRA).astype(F32)
        lanes = lax.broadcasted_iota(jnp.int32, (256, EXTRA), 1)
        chosen = (lanes == index) | (lanes == index + 16)
        share = jnp.sum(jnp.where(chosen, table, 0.0), axis=-1, keepdims=True)

        @pl.loop(0, 16)
        def _(n):
            right = w[:, pl.ds(pl.multiple_of(2 * FF + n * 48, 16), 48)].reshape(FF, 256)
            part = jnp.dot(act[...], right, preferred_element_type=F32) * share
            cols = pl.ds(pl.multiple_of(n * 256, 256), 256)
            y[r, :, :, :, cols] = part.astype(BF16).reshape(2, 4, HALF, 256)

    feed(3)
    downs.wait()
    down(3)
    scatter.start(3)
    feed(2)
    down(2)
    scatter.start(2)
    scatter.middle(3)
    feed(1)
    down(1)
    scatter.start(1)
    scatter.middle(2)
    scatter.finish(3)
    scatter.start(4)
    feed(0)
    scatter.middle(1)
    scatter.finish(2)
    down(0)
    scatter.start(0)
    scatter.finish(1)
    scatter.middle(4)
    scatter.middle(0)
    scatter.finish(0)
    for half in (0, 1):
        rows = slice(half * HALF, (half + 1) * HALF)
        out[rows] = (residual[rows] + scatter.total(half)).astype(BF16)
    scatter.drain()


def rope_tables():
    frequency = np.exp(np.arange(HD // 2, dtype=np.float32) * np.float32(-2.0 * math.log(1000000.0) / HD))
    angles = (np.arange(SEQ, dtype=np.float32)[:, None] * frequency[None, :]).astype(np.float32)
    cosine, sine = np.cos(angles), np.sin(angles)
    return (
        np.concatenate([cosine, cosine], axis=1).astype(np.float32),
        np.concatenate([-sine, sine], axis=1).astype(np.float32),
    )


VMEM = pl.BlockSpec(memory_space=pltpu.VMEM)
ANY = pl.BlockSpec(memory_space=pl.ANY)
HBM = pl.BlockSpec(memory_space=pltpu.HBM)
SEMS = pltpu.SemaphoreType.DMA((40,))
RING = [
    pltpu.VMEM((4, 2, 4, HALF, D), BF16),
    pltpu.VMEM((2, 5, 2, 16, D), BF16),
    pltpu.VMEM((2, 5, 2, HALF, D), BF16),
    pltpu.VMEM((2, 4, HALF, D), BF16),
]


def params(number, mib):
    return pltpu.CompilerParams(collective_id=number, has_side_effects=True, vmem_limit_bytes=mib * MIB)


def cost(flops, moved):
    return pl.CostEstimate(flops=flops, bytes_accessed=moved, transcendentals=0)


def local(
    tokens,
    attn_gain,
    moe_gain,
    w_query,
    w_key,
    w_value,
    w_out,
    expert_gate,
    expert_up,
    expert_down,
    routes,
    route_weights,
):
    groups = lax.axis_size("expert")
    column = lax.axis_index("expert")
    key_heads = w_key.shape[1] // HD
    key_start = column * key_heads // groups * HD
    rows = tokens[0]
    key_cols = lax.dynamic_slice_in_dim(w_key, key_start, HD, 1)
    value_cols = lax.dynamic_slice_in_dim(w_value, key_start, HD, 1)
    attn_shard = jnp.concatenate([w_query, jnp.concatenate([key_cols, value_cols], axis=1), w_out], axis=0)
    attn_weights = lax.all_gather(attn_shard, "dp", axis=0)
    gathered, extra, moe_shard = pl.pallas_call(
        gather_kernel,
        out_shape=(
            jax.ShapeDtypeStruct((16, TOK, D), BF16),
            jax.ShapeDtypeStruct((TOK, EXTRA), BF16),
            jax.ShapeDtypeStruct((2304, 256), BF16),
        ),
        in_specs=[VMEM] * 4 + [ANY] * 3,
        out_specs=(HBM, VMEM, HBM),
        scratch_shapes=[
            pltpu.VMEM((TOK, D), BF16),
            SEMS,
            SEMS,
            pltpu.SemaphoreType.DMA,
            pltpu.SemaphoreType.DMA((22,)),
        ],
        compiler_params=params(0, 60),
        cost_estimate=cost(1 << 22, 100 * MIB),
        name="gather_tokens",
    )(rows, attn_gain[None], routes[0], route_weights[0], expert_gate[0], expert_up[0], expert_down[0])

    moe_shard, attn_weights = lax.optimization_barrier((moe_shard, attn_weights))
    moe_weights = lax.all_gather(moe_shard, "dp", axis=0)
    cosine, sine = rope_tables()

    residual, everyone = pl.pallas_call(
        attend,
        out_shape=(
            jax.ShapeDtypeStruct((TOK, D), F32),
            jax.ShapeDtypeStruct((4, 2, 4, HALF, D + EXTRA), BF16),
        ),
        in_specs=[ANY, ANY, VMEM, VMEM, VMEM, VMEM, VMEM],
        out_specs=(VMEM, HBM),
        scratch_shapes=[
            pltpu.VMEM((16, TOK, D), BF16),
            pltpu.VMEM((16, 768, 256), BF16),
            pltpu.VMEM((2, SEQ, HD), BF16),
            pltpu.VMEM((SEQ, HD), BF16),
            pltpu.VMEM((SEQ, HD), BF16),
            pltpu.VMEM((16, TOK, 256), BF16),
            pltpu.VMEM((TOK, D + EXTRA), BF16),
            *RING,
            SEMS,
            SEMS,
            SEMS,
            SEMS,
            pltpu.SemaphoreType.DMA((2,)),
        ],
        compiler_params=params(1, 56),
        cost_estimate=cost(8 << 30, 150 * MIB),
        name="attention",
    )(gathered, attn_weights, rows, cosine, sine, moe_gain[None], extra)

    layer_out = pl.pallas_call(
        experts,
        out_shape=jax.ShapeDtypeStruct((TOK, D), BF16),
        in_specs=[ANY, ANY, VMEM],
        out_specs=VMEM,
        scratch_shapes=[
            pltpu.VMEM((4, 2, 4, HALF, D + EXTRA), BF16),
            pltpu.VMEM((16, 2304, 256), BF16),
            pltpu.VMEM((256, FF), BF16),
            *RING,
            SEMS,
            SEMS,
            pltpu.SemaphoreType.DMA((4,)),
            pltpu.SemaphoreType.DMA((6,)),
            pltpu.SemaphoreType.DMA,
        ],
        compiler_params=params(2, 60),
        cost_estimate=cost(20 << 30, 200 * MIB),
        name="experts",
    )(everyone, moe_weights, residual)
    return layer_out[None]


def solution(mesh):
    return jax.shard_map(
        local,
        mesh=mesh,
        in_specs=(
            P("dp", "expert", None),
            P(),
            P(),
            P("dp", "expert"),
            P("dp", None),
            P("dp", None),
            P("expert", "dp"),
            P("expert", "dp", None),
            P("expert", "dp", None),
            P("expert", "dp", None),
            P("dp", "expert", None),
            P("dp", "expert", None),
        ),
        out_specs=P("dp", "expert", None),
        check_vma=False,
    )
```

```python
import functools
import math

import jax
import jax.numpy as jnp
import numpy as np
from jax import lax
from jax.experimental import pallas as pl
from jax.experimental.pallas import tpu as pltpu
from jax.sharding import PartitionSpec as P

HD = 128
D = 4096
FF = 768
TOK = 64
HALF = 32
SEQ = 1024
EXTRA = 128
MESH = pl.DeviceIdType.MESH
F32 = jnp.float32
BF16 = jnp.bfloat16
MIB = 1 << 20

STEP = (0, 3, 1, 2)


def place():
    index = lax.axis_index("expert")
    x, y = index // 4, index % 4
    return (
        (x, y, lambda first, second: {"expert": first * 4 + second}),
        (y, x, lambda first, second: {"expert": second * 4 + first}),
    )


def turn(coordinate, step):
    return (coordinate + step) % 4


def around(spots):
    return [device(turn(f, step), s) for f, s, device in spots for step in (1, 3)]


def meet(devices):
    barrier = pltpu.get_barrier_semaphore()
    for device in devices:
        pl.semaphore_signal(barrier, inc=1, device_id=device, device_id_type=MESH)
    pl.semaphore_wait(barrier, len(devices))


def remote(source, target, sends, recvs, slot, device):
    copy = pltpu.make_async_remote_copy(
        src_ref=source,
        dst_ref=target,
        send_sem=sends.at[slot],
        recv_sem=recvs.at[slot],
        device_id=device,
        device_id_type=MESH,
    )
    copy.start()
    return copy


class Gather:
    def __init__(self, spots, block, sends, recvs, own, absolute):
        self.spots, self.block, self.sends, self.recvs = spots, block, sends, recvs
        self.own, self.absolute = own, absolute
        self.copies = {}

    def send(self, half, group, lane, source, target, device):
        slot = (half * 5 + group) * 4 + lane
        self.copies[half, group, lane] = remote(
            source, target, self.sends, self.recvs, slot, device
        )

    def first_hop(self):
        for half, (f, s, device) in enumerate(self.spots):
            for lane, step in ((0, 1), (1, 3)):
                target = self.block(0 if self.absolute else 1 + lane, half, s, 0, HALF)
                self.send(half, 4, lane, self.own(half), target, device(turn(f, step), s))
        self.spread(0)

    def spread(self, r, halves=(0, 1)):
        for half in halves:
            f, s, device = self.spots[half]
            mine = self.own(half) if r == 0 else self.block(r, half, s, 0, HALF)
            for lane, step in ((0, 1), (1, 3)):
                self.send(half, r, lane, mine, self.block(r, half, s, 0, HALF), device(f, turn(s, step)))

    def second_hop(self):
        for lane, step in ((0, 1), (1, 3)):
            for half, (f, s, device) in enumerate(self.spots):
                self.copies[half, 4, lane].wait_recv()
                source = self.block(1 + lane, half, s, lane * 16, 16)
                target = source if self.absolute else self.block(3, half, s, lane * 16, 16)
                self.send(half, 4, 2 + lane, source, target, device(turn(f, step), s))
                self.spread(1 + lane, (half,))

    def last_hop(self):
        for half in (0, 1):
            for lane in (2, 3):
                self.copies[half, 4, lane].wait_recv()
            self.spread(3, (half,))

    def forward(self, r):
        for lane, step in ((0, 1), (1, 3)):
            for half, (f, s, device) in enumerate(self.spots):
                self.copies[half, r, lane].wait_recv()
                here = self.block(r, half, turn(s, 4 - step), lane * 16, 16)
                self.send(half, r, 2 + lane, here, here, device(f, turn(s, step)))

    def finish(self, r):
        for half in (0, 1):
            for lane in (2, 3):
                self.copies[half, r, lane].wait_recv()

    def rest(self):
        self.second_hop()
        self.forward(0)
        self.last_hop()
        for r in (1, 2, 3):
            self.forward(r)
        for r in range(4):
            self.finish(r)
        self.drain()

    def drain(self):
        for copy in self.copies.values():
            copy.wait_send()


class Scatter:
    def __init__(self, spots, y_ref, small, large, z_ref, sends, recvs, cut=HALF // 2):
        self.spots, self.y, self.small, self.large, self.z = spots, y_ref, small, large, z_ref
        self.sends, self.recvs, self.cut = sends, recvs, cut
        self.copies = {}

    def send(self, half, group, lane, source, target, device):
        slot = (half * 5 + group) * 4 + lane
        self.copies[half, group, lane] = remote(
            source, target, self.sends, self.recvs, slot, device
        )

    def parts(self, half, group):
        f, s, device = self.spots[half]
        if group < 4:
            return (
                lambda step: self.y.at[group, half, turn(s, step)],
                lambda step: device(f, turn(s, step)),
            )
        return (
            lambda step: self.z.at[half, STEP.index(step)],
            lambda step: device(turn(f, step), s),
        )

    def start(self, group):
        for half in (0, 1):
            block, device = self.parts(half, group)
            for lane, step in ((0, 1), (1, 3)):
                self.send(
                    half, group, lane, block(2).at[pl.ds(lane * self.cut, self.cut)], self.small.at[half, group, lane],
                    device(step),
                )

    def middle(self, group):
        for lane, step in ((0, 1), (1, 3)):
            for half in (0, 1):
                block, device = self.parts(half, group)
                self.copies[half, group, lane].wait_recv()
                rows = block(step).at[pl.ds(lane * self.cut, self.cut)]
                rows[...] = (rows[...].astype(F32) + self.small[half, group, lane].astype(F32)).astype(BF16)
                self.send(half, group, 2 + lane, block(step), self.large.at[half, group, lane], device(step))

    def arrived(self, half, group):
        for lane in (2, 3):
            self.copies[half, group, lane].wait_recv()
        return self.large[half, group, 0].astype(F32) + self.large[half, group, 1].astype(F32)

    def finish(self, group):
        for half in (0, 1):
            _, s, _ = self.spots[half]
            total = self.arrived(half, group) + self.y[group, half, s].astype(F32)
            self.z[half, group] = total.astype(BF16)

    def total(self, half):
        return self.arrived(half, 4) + self.z[half, 0].astype(F32)

    def drain(self):
        for copy in self.copies.values():
            copy.wait_send()


class Fold(Scatter):
    def parts(self, half, group):
        f, s, device = self.spots[half]
        return (lambda step: self.y.at[half, turn(f, step)], lambda step: device(turn(f, step), s))

    def total(self, half):
        return self.arrived(half, 0) + self.y[half, self.spots[half][0]].astype(F32)


def normalized(values, gain):
    return values * lax.rsqrt(jnp.mean(values * values, axis=-1, keepdims=True) + 1e-06) * gain


def pack_kernel(gate, up, down, w_query, w_key, w_value, w_out, attn_shard, moe_shard):
    key_cols = pl.ds(pl.multiple_of(lax.axis_index("expert") // 8 * HD, HD), HD)
    attn_shard[0:256] = w_query[...]
    attn_shard[256:512, 0:HD] = w_key[:, key_cols]
    attn_shard[256:512, HD:] = w_value[:, key_cols]
    attn_shard[512:768] = w_out[...]
    for c in range(3):
        cols = slice(c * 256, c * 256 + 256)
        moe_shard[cols] = gate[:, cols]
        moe_shard[FF + c * 256 : FF + c * 256 + 256] = up[:, cols]
    for c in range(16):
        moe_shard[2 * FF + c * 48 : 2 * FF + c * 48 + 48] = down[:, c * 256 : c * 256 + 256]


def gather_kernel(
    tokens, gain, routes, weights,
    out, extra,
    own, sends, recvs, local,
):
    spots = place()
    index = lax.axis_index("expert")
    own[...] = normalized(tokens[...].astype(F32), gain[...]).astype(BF16)
    keep = pltpu.make_async_copy(own, out.at[index], local)
    keep.start()
    meet(around(spots))

    def block(r, half, second, start, rows):
        f, _, device = spots[half]
        return out.at[device(turn(f, STEP[r]), second)["expert"], pl.ds(half * HALF + start, rows)]

    gather = Gather(spots, block, sends, recvs, lambda half: own.at[pl.ds(half * HALF, HALF)], True)
    gather.first_hop()

    share = weights[...] / jnp.sum(weights[...], axis=0, keepdims=True)
    high = share.astype(BF16).astype(F32)
    low = share - high
    at_row = lax.broadcasted_iota(jnp.int32, (EXTRA, TOK), 0)
    table = jnp.zeros((EXTRA, TOK), F32)
    for k in range(routes.shape[0]):
        named = routes[k : k + 1]
        table += jnp.where(at_row == named, high[k : k + 1], 0.0)
        table += jnp.where(at_row == named + 16, low[k : k + 1], 0.0)
    extra[...] = table.T.astype(BF16)

    gather.rest()
    keep.wait()


class Share:
    def __init__(self, spots, weights, wo, sends, recvs):
        index = lax.axis_index("dp")
        self.core = index % 2
        self.other = {"dp": index + 1 - 2 * self.core}
        self.spots, self.weights, self.wo, self.sends, self.recvs = spots, weights, wo, sends, recvs
        self.copies = {}

    def block(self, half, second, start, count):
        return self.wo.at[half, pl.ds(4 * self.core + start, count), second]

    def send(self, half, lane, source, target, device):
        self.copies[half, lane] = remote(source, target, self.sends, self.recvs, half * 8 + lane, device)

    def start(self):
        for half, (f, s, device) in enumerate(self.spots):
            source = self.weights.at[pl.ds(8 * half + 4 * self.core, 4), pl.ds(512, 256)]
            for lane, step in ((0, 1), (1, 3)):
                self.send(half, lane, source, self.block(half, s, 0, 4), device(f, turn(s, step)))

    def forward(self):
        for lane, step in ((0, 1), (1, 3)):
            for half, (f, s, device) in enumerate(self.spots):
                self.copies[half, lane].wait_recv()
                here = self.block(half, turn(s, 4 - step), 2 * lane, 2)
                self.send(half, 2 + lane, here, here, device(f, turn(s, step)))
                here = self.block(half, turn(s, 4 - step), 0, 4)
                self.send(half, 4 + lane, here, here, self.other)

    def finish(self):
        for lane in (0, 1):
            for half, (f, s, device) in enumerate(self.spots):
                self.copies[half, 2 + lane].wait_recv()
                here = self.block(half, turn(s, 2), 2 * lane, 2)
                self.send(half, 6 + lane, here, here, self.other)

    def arrive(self):
        for half in (0, 1):
            for lane in range(4, 8):
                self.copies[half, lane].wait_recv()

    def drain(self):
        for copy in self.copies.values():
            copy.wait_send()


def attend(
    gathered, weights, tokens, cosine, sine, gain, extra,
    residual, everyone,
    x, w, wo, queries, keys, values, mixed, mx, moe_in, y, small, large,
    wo_sends, wo_recvs, mx_sends, mx_recvs, sends, recvs, out_sends, out_recvs, local,
):
    spots = place()
    load_w = pltpu.make_async_copy(weights.at[:, pl.ds(0, 512)], w, local.at[0])
    load_w.start()
    loads = []
    for i in range(4):
        loads.append(pltpu.make_async_copy(gathered.at[pl.ds(i * 4, 4)], x.at[pl.ds(i * 4, 4)], local.at[1 + i]))
        loads[-1].start()
    for half, (f, s, _) in enumerate(spots):
        loads.append(
            pltpu.make_async_copy(
                weights.at[pl.ds(8 * half, 8), pl.ds(512, 256)], wo.at[half, :, s], local.at[5 + half]
            )
        )
        loads[-1].start()
    share = Share(spots, weights, wo, wo_sends, wo_recvs)
    across = [device(f, turn(s, 2)) for f, s, device in spots]
    meet(around(spots) + across + [share.other])
    share.start()
    load_w.wait()

    def rope(part, rows):
        return part * cosine[rows] + pltpu.roll(part, HD // 2, 1) * sine[rows]

    def project(i):
        loads[i].wait()
        rows = slice(i * 256, i * 256 + 256)
        left = x[i * 4 : i * 4 + 4].reshape(256, D)
        q = jnp.dot(left, w[:, 0:256].reshape(D, 256), preferred_element_type=F32)
        for head in (0, 1):
            queries[head, rows] = rope(q[:, head * HD : (head + 1) * HD], rows).astype(BF16)
        kv = jnp.dot(left, w[:, 256:512].reshape(D, 256), preferred_element_type=F32)
        keys[rows] = rope(kv[:, :HD], rows).astype(BF16)
        values[rows] = kv[:, HD:].astype(BF16)

    def attention(i):
        many = (i + 1) * 256
        for head in (0, 1):
            scores = lax.dot_general(
                queries[head, i * 256 : many], keys[0:many], (((1,), (1,)), ((), ())), preferred_element_type=F32
            ) * (1.0 / math.sqrt(HD))
            at_row = lax.broadcasted_iota(jnp.int32, (256, many), 0) + i * 256
            at_col = lax.broadcasted_iota(jnp.int32, (256, many), 1)
            scores = jnp.where(at_row >= at_col, scores, -1e30)
            grown = jnp.exp(scores - jnp.max(scores, axis=-1, keepdims=True))
            total = jnp.sum(grown, axis=-1, keepdims=True)
            part = jnp.dot(grown.astype(BF16), values[0:many], preferred_element_type=F32) / total
            mixed[i, :, :, head * HD : (head + 1) * HD] = part.astype(BF16).reshape(4, TOK, HD)

    for i in range(4):
        project(i)
    share.forward()
    for i in range(4):
        attention(i)

    def rows_of(half, second):
        return mixed.at[second] if half else mixed.at[:, second]

    swaps = []
    for i, step in enumerate((1, 3, 2)):
        for half, (f, s, device) in enumerate(spots):
            cols = pl.ds(pl.multiple_of(s * 256, 256), 256)
            to = turn(s, step)
            swaps.append(
                remote(rows_of(half, to), mx.at[half, :, :, cols], mx_sends, mx_recvs, half * 3 + i, device(f, to))
            )
    keeps = []
    for half, (f, s, device) in enumerate(spots):
        cols = pl.ds(pl.multiple_of(s * 256, 256), 256)
        keeps.append(pltpu.make_async_copy(rows_of(half, s), mx.at[half, :, :, cols], local.at[half]))
        keeps[-1].start()
    share.finish()
    for copy in keeps + loads[4:]:
        copy.wait()
    for copy in swaps:
        copy.wait_recv()
    share.arrive()

    fold = Fold(spots, y, small, large, None, sends, recvs, HALF)
    for half in (0, 1):

        @pl.loop(0, 2)
        def _(group):
            left = mx[half].reshape(256, 1024)
            for c in range(4):
                right = wo[half, group * 4 + c].reshape(1024, 256)
                part = jnp.dot(left, right, preferred_element_type=F32)
                cols = pl.ds(pl.multiple_of(group * 1024 + c * 256, 256), 256)
                y[half, :, :, cols] = part.astype(BF16).reshape(4, TOK, 256)

    fold.start(0)
    for copy in swaps:
        copy.wait_send()
    share.drain()
    fold.middle(0)
    for half in (0, 1):
        cols = slice(half * 2048, (half + 1) * 2048)
        residual[:, cols] = tokens[:, cols].astype(F32) + fold.total(half)
    moe_in[:, 0:D] = normalized(residual[...], gain[...]).astype(BF16)
    moe_in[:, D:] = extra[...]

    def block(r, half, second, start, rows):
        return everyone.at[r, half, second, pl.ds(start, rows)]

    gather = Gather(spots, block, out_sends, out_recvs, lambda half: moe_in.at[pl.ds(half * HALF, HALF)], False)
    gather.first_hop()
    keeps = []
    for half, (_, s, _) in enumerate(spots):
        keeps.append(pltpu.make_async_copy(gather.own(half), block(0, half, s, 0, HALF), local.at[half]))
        keeps[-1].start()
    fold.drain()
    gather.rest()
    for keep in keeps:
        keep.wait()


def experts(
    everyone, weights, residual,
    out,
    g, w, act, y, small, large, z, sends, recvs, load_g, load_w, load_down,
):
    spots = place()
    rows_of = [pltpu.make_async_copy(everyone.at[r], g.at[r], load_g.at[r]) for r in range(4)]
    feeds = []
    for c in range(6):
        part = (c // 2 + c % 2 * 3) * 256
        view = pl.ds(part, 256)
        feeds.append(pltpu.make_async_copy(weights.at[:, view], w.at[:, view], load_w.at[c]))
    view = pl.ds(2 * FF, FF)
    downs = pltpu.make_async_copy(weights.at[:, view], w.at[:, view], load_down)
    rows_of[3].start()
    for copy in feeds:
        copy.start()
    for r in (2, 1, 0):
        rows_of[r].start()
    downs.start()
    meet(around(spots))
    scatter = Scatter(spots, y, small, large, z, sends, recvs)
    index = lax.axis_index("expert")

    def feed_part(r, c):
        cols = pl.ds(c * 256, 256)
        left = g[r, :, :, :, 0:D].reshape(256, D)
        gate = jnp.dot(left, w[:, cols].reshape(D, 256), preferred_element_type=F32)
        up = jnp.dot(left, w[:, pl.ds(FF + c * 256, 256)].reshape(D, 256), preferred_element_type=F32)
        act[:, cols] = (gate / (1.0 + jnp.exp(-gate)) * up).astype(BF16)

    def feed(r):
        rows_of[r].wait()
        for c in range(3):
            if r == 3:
                feeds[2 * c].wait()
                feeds[2 * c + 1].wait()
            feed_part(r, c)

    def down(r):
        table = g[r, :, :, :, D:].reshape(256, EXTRA).astype(F32)
        lanes = lax.broadcasted_iota(jnp.int32, (256, EXTRA), 1)
        chosen = (lanes == index) | (lanes == index + 16)
        share = jnp.sum(jnp.where(chosen, table, 0.0), axis=-1, keepdims=True)

        @pl.loop(0, 4)
        def _(group):
            for c in range(4):
                n = group * 4 + c
                right = w[:, pl.ds(pl.multiple_of(2 * FF + n * 48, 16), 48)].reshape(FF, 256)
                part = jnp.dot(act[...], right, preferred_element_type=F32) * share
                cols = pl.ds(pl.multiple_of(n * 256, 256), 256)
                y[r, :, :, :, cols] = part.astype(BF16).reshape(2, 4, HALF, 256)

    feed(3)
    downs.wait()
    down(3)
    scatter.start(3)
    feed(2)
    down(2)
    scatter.start(2)
    scatter.middle(3)
    feed(1)
    down(1)
    scatter.start(1)
    scatter.middle(2)
    scatter.finish(3)
    scatter.start(4)
    feed(0)
    scatter.middle(1)
    scatter.finish(2)
    down(0)
    scatter.start(0)
    scatter.finish(1)
    scatter.middle(4)
    scatter.middle(0)
    scatter.finish(0)
    for half in (0, 1):
        rows = slice(half * HALF, (half + 1) * HALF)
        out[rows] = (residual[rows] + scatter.total(half)).astype(BF16)
    scatter.drain()


def rope_tables():
    frequency = np.exp(np.arange(HD // 2, dtype=np.float32) * np.float32(-2.0 * math.log(1000000.0) / HD))
    angles = (np.arange(SEQ, dtype=np.float32)[:, None] * frequency[None, :]).astype(np.float32)
    cosine, sine = np.cos(angles), np.sin(angles)
    return (
        np.concatenate([cosine, cosine], axis=1).astype(np.float32),
        np.concatenate([-sine, sine], axis=1).astype(np.float32),
    )


VMEM = pl.BlockSpec(memory_space=pltpu.VMEM)
ANY = pl.BlockSpec(memory_space=pl.ANY)
HBM = pl.BlockSpec(memory_space=pltpu.HBM)
SEMS = pltpu.SemaphoreType.DMA((40,))
RING = [
    pltpu.VMEM((4, 2, 4, HALF, D), BF16),
    pltpu.VMEM((2, 5, 2, 16, D), BF16),
    pltpu.VMEM((2, 5, 2, HALF, D), BF16),
    pltpu.VMEM((2, 4, HALF, D), BF16),
]


def params(number, mib):
    return pltpu.CompilerParams(collective_id=number, has_side_effects=True, vmem_limit_bytes=mib * MIB)


def cost(flops, moved):
    return pl.CostEstimate(flops=flops, bytes_accessed=moved, transcendentals=0)


def local(
    tokens,
    attn_gain,
    moe_gain,
    w_query,
    w_key,
    w_value,
    w_out,
    expert_gate,
    expert_up,
    expert_down,
    routes,
    route_weights,
):
    rows = tokens[0]
    attn_shard, moe_shard = pl.pallas_call(
        pack_kernel,
        out_shape=(jax.ShapeDtypeStruct((768, 256), BF16), jax.ShapeDtypeStruct((2304, 256), BF16)),
        in_specs=[VMEM] * 7,
        out_specs=(VMEM, VMEM),
        compiler_params=pltpu.CompilerParams(vmem_limit_bytes=60 * MIB),
        cost_estimate=cost(1 << 10, 4 * MIB),
        name="pack_weights",
    )(expert_gate[0], expert_up[0], expert_down[0], w_query, w_key, w_value, w_out)
    attn_weights = lax.all_gather(attn_shard, "dp", axis=0)
    moe_weights = lax.all_gather(moe_shard, "dp", axis=0)

    gathered, extra = pl.pallas_call(
        gather_kernel,
        out_shape=(jax.ShapeDtypeStruct((16, TOK, D), BF16), jax.ShapeDtypeStruct((TOK, EXTRA), BF16)),
        in_specs=[VMEM] * 4,
        out_specs=(HBM, VMEM),
        scratch_shapes=[pltpu.VMEM((TOK, D), BF16), SEMS, SEMS, pltpu.SemaphoreType.DMA],
        compiler_params=params(0, 60),
        cost_estimate=cost(1 << 10, MIB),
        name="gather_tokens",
    )(rows, attn_gain[None], routes[0].T, route_weights[0].T)

    cosine, sine = rope_tables()
    residual, everyone = pl.pallas_call(
        attend,
        out_shape=(
            jax.ShapeDtypeStruct((TOK, D), F32),
            jax.ShapeDtypeStruct((4, 2, 4, HALF, D + EXTRA), BF16),
        ),
        in_specs=[ANY, ANY, VMEM, VMEM, VMEM, VMEM, VMEM],
        out_specs=(VMEM, HBM),
        scratch_shapes=[
            pltpu.VMEM((16, TOK, D), BF16),
            pltpu.VMEM((16, 512, 256), BF16),
            pltpu.VMEM((2, 8, 4, 256, 256), BF16),
            pltpu.VMEM((2, SEQ, HD), BF16),
            pltpu.VMEM((SEQ, HD), BF16),
            pltpu.VMEM((SEQ, HD), BF16),
            pltpu.VMEM((4, 4, TOK, 256), BF16),
            pltpu.VMEM((2, 4, TOK, 1024), BF16),
            pltpu.VMEM((TOK, D + EXTRA), BF16),
            pltpu.VMEM((2, 4, TOK, 2048), BF16),
            pltpu.VMEM((2, 1, 2, HALF, 2048), BF16),
            pltpu.VMEM((2, 1, 2, TOK, 2048), BF16),
            pltpu.SemaphoreType.DMA((16,)),
            pltpu.SemaphoreType.DMA((16,)),
            pltpu.SemaphoreType.DMA((6,)),
            pltpu.SemaphoreType.DMA((6,)),
            SEMS,
            SEMS,
            SEMS,
            SEMS,
            pltpu.SemaphoreType.DMA((7,)),
        ],
        compiler_params=params(1, 56),
        cost_estimate=cost(1 << 10, MIB),
        name="attention",
    )(gathered, attn_weights, rows, cosine, sine, moe_gain[None], extra)

    layer_out = pl.pallas_call(
        experts,
        out_shape=jax.ShapeDtypeStruct((TOK, D), BF16),
        in_specs=[ANY, ANY, VMEM],
        out_specs=VMEM,
        scratch_shapes=[
            pltpu.VMEM((4, 2, 4, HALF, D + EXTRA), BF16),
            pltpu.VMEM((16, 2304, 256), BF16),
            pltpu.VMEM((256, FF), BF16),
            *RING,
            SEMS,
            SEMS,
            pltpu.SemaphoreType.DMA((4,)),
            pltpu.SemaphoreType.DMA((6,)),
            pltpu.SemaphoreType.DMA,
        ],
        compiler_params=params(2, 60),
        cost_estimate=cost(20 << 30, 200 * MIB),
        name="experts",
    )(everyone, moe_weights, residual)
    return layer_out[None]


def solution(mesh):
    return jax.shard_map(
        local,
        mesh=mesh,
        in_specs=(
            P("dp", "expert", None),
            P(),
            P(),
            P("dp", "expert"),
            P("dp", None),
            P("dp", None),
            P("expert", "dp"),
            P("expert", "dp", None),
            P("expert", "dp", None),
            P("expert", "dp", None),
            P("dp", "expert", None),
            P("dp", "expert", None),
        ),
        out_specs=P("dp", "expert", None),
        check_vma=False,
    )
```

```python
import functools
import math

import jax
import jax.numpy as jnp
import numpy as np
from jax import lax
from jax.experimental import pallas as pl
from jax.experimental.pallas import tpu as pltpu
from jax.sharding import PartitionSpec as P

HD = 128
D = 4096
FF = 768
TOK = 64
HALF = 32
SEQ = 1024
EXTRA = 128
MESH = pl.DeviceIdType.MESH
F32 = jnp.float32
BF16 = jnp.bfloat16
MIB = 1 << 20

STEP = (0, 3, 1, 2)


def place():
    index = lax.axis_index("expert")
    x, y = index // 4, index % 4
    return (
        (x, y, lambda first, second: {"expert": first * 4 + second}),
        (y, x, lambda first, second: {"expert": second * 4 + first}),
    )


def turn(coordinate, step):
    return (coordinate + step) % 4


def around(spots):
    return [device(turn(f, step), s) for f, s, device in spots for step in (1, 3)]


def meet(devices):
    barrier = pltpu.get_barrier_semaphore()
    for device in devices:
        pl.semaphore_signal(barrier, inc=1, device_id=device, device_id_type=MESH)
    pl.semaphore_wait(barrier, len(devices))


def remote(source, target, sends, recvs, slot, device):
    copy = pltpu.make_async_remote_copy(
        src_ref=source,
        dst_ref=target,
        send_sem=sends.at[slot],
        recv_sem=recvs.at[slot],
        device_id=device,
        device_id_type=MESH,
    )
    copy.start()
    return copy


class Gather:
    def __init__(self, spots, block, sends, recvs, own, absolute):
        self.spots, self.block, self.sends, self.recvs = spots, block, sends, recvs
        self.own, self.absolute = own, absolute
        self.copies = {}

    def send(self, half, group, lane, source, target, device):
        slot = (half * 5 + group) * 4 + lane
        self.copies[half, group, lane] = remote(
            source, target, self.sends, self.recvs, slot, device
        )

    def first_hop(self):
        for half, (f, s, device) in enumerate(self.spots):
            for lane, step in ((0, 1), (1, 3)):
                target = self.block(0 if self.absolute else 1 + lane, half, s, 0, HALF)
                self.send(half, 4, lane, self.own(half), target, device(turn(f, step), s))
        self.spread(0)

    def spread(self, r, halves=(0, 1)):
        for half in halves:
            f, s, device = self.spots[half]
            mine = self.own(half) if r == 0 else self.block(r, half, s, 0, HALF)
            for lane, step in ((0, 1), (1, 3)):
                self.send(half, r, lane, mine, self.block(r, half, s, 0, HALF), device(f, turn(s, step)))

    def second_hop(self):
        for lane, step in ((0, 1), (1, 3)):
            for half, (f, s, device) in enumerate(self.spots):
                self.copies[half, 4, lane].wait_recv()
                source = self.block(1 + lane, half, s, lane * 16, 16)
                target = source if self.absolute else self.block(3, half, s, lane * 16, 16)
                self.send(half, 4, 2 + lane, source, target, device(turn(f, step), s))
                self.spread(1 + lane, (half,))

    def last_hop(self):
        for half in (0, 1):
            for lane in (2, 3):
                self.copies[half, 4, lane].wait_recv()
            self.spread(3, (half,))

    def forward(self, r):
        for lane, step in ((0, 1), (1, 3)):
            for half, (f, s, device) in enumerate(self.spots):
                self.copies[half, r, lane].wait_recv()
                here = self.block(r, half, turn(s, 4 - step), lane * 16, 16)
                self.send(half, r, 2 + lane, here, here, device(f, turn(s, step)))

    def finish(self, r):
        for half in (0, 1):
            for lane in (2, 3):
                self.copies[half, r, lane].wait_recv()

    def rest(self):
        self.second_hop()
        self.forward(0)
        self.last_hop()
        for r in (1, 2, 3):
            self.forward(r)
        for r in range(4):
            self.finish(r)
        self.drain()

    def drain(self):
        for copy in self.copies.values():
            copy.wait_send()


class Scatter:
    def __init__(self, spots, y_ref, small, large, z_ref, sends, recvs, cut=HALF // 2):
        self.spots, self.y, self.small, self.large, self.z = spots, y_ref, small, large, z_ref
        self.sends, self.recvs, self.cut = sends, recvs, cut
        self.copies = {}

    def send(self, half, group, lane, source, target, device):
        slot = (half * 5 + group) * 4 + lane
        self.copies[half, group, lane] = remote(
            source, target, self.sends, self.recvs, slot, device
        )

    def parts(self, half, group):
        f, s, device = self.spots[half]
        if group < 4:
            return (
                lambda step: self.y.at[group, half, turn(s, step)],
                lambda step: device(f, turn(s, step)),
            )
        return (
            lambda step: self.z.at[half, STEP.index(step)],
            lambda step: device(turn(f, step), s),
        )

    def start(self, group):
        for half in (0, 1):
            block, device = self.parts(half, group)
            for lane, step in ((0, 1), (1, 3)):
                self.send(
                    half, group, lane, block(2).at[pl.ds(lane * self.cut, self.cut)], self.small.at[half, group, lane],
                    device(step),
                )

    def middle(self, group):
        for lane, step in ((0, 1), (1, 3)):
            for half in (0, 1):
                block, device = self.parts(half, group)
                self.copies[half, group, lane].wait_recv()
                rows = block(step).at[pl.ds(lane * self.cut, self.cut)]
                rows[...] = (rows[...].astype(F32) + self.small[half, group, lane].astype(F32)).astype(BF16)
                self.send(half, group, 2 + lane, block(step), self.large.at[half, group, lane], device(step))

    def arrived(self, half, group):
        for lane in (2, 3):
            self.copies[half, group, lane].wait_recv()
        return self.large[half, group, 0].astype(F32) + self.large[half, group, 1].astype(F32)

    def finish(self, group):
        for half in (0, 1):
            _, s, _ = self.spots[half]
            total = self.arrived(half, group) + self.y[group, half, s].astype(F32)
            self.z[half, group] = total.astype(BF16)

    def total(self, half):
        return self.arrived(half, 4) + self.z[half, 0].astype(F32)

    def drain(self):
        for copy in self.copies.values():
            copy.wait_send()


class Fold(Scatter):
    def parts(self, half, group):
        f, s, device = self.spots[half]
        return (lambda step: self.y.at[half, turn(f, step)], lambda step: device(turn(f, step), s))

    def total(self, half):
        return self.arrived(half, 0) + self.y[half, self.spots[half][0]].astype(F32)


class Column:
    def __init__(self, mine, w_ref, sends, recvs):
        index = lax.axis_index("dp")
        self.mine, self.w, self.sends, self.recvs = mine, w_ref, sends, recvs
        self.level, self.core = index // 2, index % 2
        self.other = {"dp": self.level * 2 + 1 - self.core}
        self.next = [{"dp": (self.level + step) % 8 * 2 + self.core} for step in (1, 7)]
        self.copies = {}

    def send(self, slot, step, device, way=None):
        start, rows = (0, 768) if way is None else (way * 384, 384)
        place = self.w.at[(self.level + step) % 8 * 2 + self.core, pl.ds(start, rows)]
        source = place if step else self.mine
        self.copies[slot] = remote(source, place, self.sends, self.recvs, slot, device)

    def start(self):
        for way in (0, 1):
            self.send(way * 4, 0, self.next[way])
        self.send(8, 0, self.other)

    def step(self, t):
        for way in (0, 1):
            self.copies[way * 4 + t - 1].wait_recv()
            here = t if way else 8 - t
            if t < 4:
                self.send(way * 4 + t, here, self.next[way], way if t == 3 else None)
            self.send(8 + way * 4 + t, here, self.other, way if t == 4 else None)

    def finish(self):
        for slot in range(8, 17):
            self.copies[slot].wait_recv()
        for copy in self.copies.values():
            copy.wait_send()


def normalized(values, gain):
    return values * lax.rsqrt(jnp.mean(values * values, axis=-1, keepdims=True) + 1e-06) * gain


def pack_kernel(gate, up, down, w_query, w_key, w_value, w_out, attn_shard, moe_shard, down_shard):
    key_cols = pl.ds(pl.multiple_of(lax.axis_index("expert") // 8 * HD, HD), HD)
    attn_shard[0:256] = w_query[...]
    attn_shard[256:512, 0:HD] = w_key[:, key_cols]
    attn_shard[256:512, HD:] = w_value[:, key_cols]
    attn_shard[512:768] = w_out[...]
    for c in range(3):
        cols = slice(c * 256, c * 256 + 256)
        moe_shard[cols] = gate[:, cols]
        moe_shard[FF + c * 256 : FF + c * 256 + 256] = up[:, cols]
    for c in range(16):
        down_shard[c * 48 : c * 48 + 48] = down[:, c * 256 : c * 256 + 256]


def gather_kernel(
    tokens, gain, routes, weights,
    out, extra,
    own, sends, recvs, local,
):
    spots = place()
    index = lax.axis_index("expert")
    own[...] = normalized(tokens[...].astype(F32), gain[...]).astype(BF16)
    keep = pltpu.make_async_copy(own, out.at[index], local)
    keep.start()
    meet(around(spots))

    def block(r, half, second, start, rows):
        f, _, device = spots[half]
        return out.at[device(turn(f, STEP[r]), second)["expert"], pl.ds(half * HALF + start, rows)]

    gather = Gather(spots, block, sends, recvs, lambda half: own.at[pl.ds(half * HALF, HALF)], True)
    gather.first_hop()

    share = weights[...] / jnp.sum(weights[...], axis=0, keepdims=True)
    high = share.astype(BF16).astype(F32)
    low = share - high
    at_row = lax.broadcasted_iota(jnp.int32, (EXTRA, TOK), 0)
    table = jnp.zeros((EXTRA, TOK), F32)
    for k in range(routes.shape[0]):
        named = routes[k : k + 1]
        table += jnp.where(at_row == named, high[k : k + 1], 0.0)
        table += jnp.where(at_row == named + 16, low[k : k + 1], 0.0)
    extra[...] = table.T.astype(BF16)

    gather.rest()
    keep.wait()


class Share:
    def __init__(self, spots, weights, wo, sends, recvs):
        index = lax.axis_index("dp")
        self.core = index % 2
        self.other = {"dp": index + 1 - 2 * self.core}
        self.spots, self.weights, self.wo, self.sends, self.recvs = spots, weights, wo, sends, recvs
        self.copies = {}

    def block(self, half, second, start, count):
        return self.wo.at[half, pl.ds(4 * self.core + start, count), second]

    def send(self, half, lane, source, target, device):
        self.copies[half, lane] = remote(source, target, self.sends, self.recvs, half * 8 + lane, device)

    def start(self):
        for half, (f, s, device) in enumerate(self.spots):
            source = self.weights.at[pl.ds(8 * half + 4 * self.core, 4), pl.ds(512, 256)]
            for lane, step in ((0, 1), (1, 3)):
                self.send(half, lane, source, self.block(half, s, 0, 4), device(f, turn(s, step)))

    def forward(self):
        for lane, step in ((0, 1), (1, 3)):
            for half, (f, s, device) in enumerate(self.spots):
                self.copies[half, lane].wait_recv()
                here = self.block(half, turn(s, 4 - step), 2 * lane, 2)
                self.send(half, 2 + lane, here, here, device(f, turn(s, step)))
                here = self.block(half, turn(s, 4 - step), 0, 4)
                self.send(half, 4 + lane, here, here, self.other)

    def finish(self):
        for lane in (0, 1):
            for half, (f, s, device) in enumerate(self.spots):
                self.copies[half, 2 + lane].wait_recv()
                here = self.block(half, turn(s, 2), 2 * lane, 2)
                self.send(half, 6 + lane, here, here, self.other)

    def arrive(self):
        for half in (0, 1):
            for lane in range(4, 8):
                self.copies[half, lane].wait_recv()

    def drain(self):
        for copy in self.copies.values():
            copy.wait_send()


def attend(
    gathered, weights, tokens, cosine, sine, gain, extra, down_shard,
    residual, everyone, down_all,
    x, w, wo, queries, keys, values, mixed, mx, moe_in, y, small, large,
    wo_sends, wo_recvs, mx_sends, mx_recvs, sends, recvs, out_sends, out_recvs, z_sends, z_recvs, local,
):
    spots = place()
    load_w = pltpu.make_async_copy(weights.at[:, pl.ds(0, 512)], w, local.at[0])
    load_w.start()
    loads = []
    for i in range(4):
        loads.append(pltpu.make_async_copy(gathered.at[pl.ds(i * 4, 4)], x.at[pl.ds(i * 4, 4)], local.at[1 + i]))
        loads[-1].start()
    for half, (f, s, _) in enumerate(spots):
        loads.append(
            pltpu.make_async_copy(
                weights.at[pl.ds(8 * half, 8), pl.ds(512, 256)], wo.at[half, :, s], local.at[5 + half]
            )
        )
        loads[-1].start()
    share = Share(spots, weights, wo, wo_sends, wo_recvs)
    across = [device(f, turn(s, 2)) for f, s, device in spots]
    column = Column(down_shard, down_all, z_sends, z_recvs)
    own_down = pltpu.make_async_copy(down_shard, down_all.at[lax.axis_index("dp")], local.at[7])
    own_down.start()
    meet(around(spots) + across + column.next + [column.other])
    share.start()
    column.start()
    load_w.wait()

    def rope(part, rows):
        return part * cosine[rows] + pltpu.roll(part, HD // 2, 1) * sine[rows]

    def project(i):
        loads[i].wait()
        rows = slice(i * 256, i * 256 + 256)
        left = x[i * 4 : i * 4 + 4].reshape(256, D)
        q = jnp.dot(left, w[:, 0:256].reshape(D, 256), preferred_element_type=F32)
        for head in (0, 1):
            queries[head, rows] = rope(q[:, head * HD : (head + 1) * HD], rows).astype(BF16)
        kv = jnp.dot(left, w[:, 256:512].reshape(D, 256), preferred_element_type=F32)
        keys[rows] = rope(kv[:, :HD], rows).astype(BF16)
        values[rows] = kv[:, HD:].astype(BF16)

    def attention(i):
        many = (i + 1) * 256
        for head in (0, 1):
            scores = lax.dot_general(
                queries[head, i * 256 : many], keys[0:many], (((1,), (1,)), ((), ())), preferred_element_type=F32
            ) * (1.0 / math.sqrt(HD))
            at_row = lax.broadcasted_iota(jnp.int32, (256, many), 0) + i * 256
            at_col = lax.broadcasted_iota(jnp.int32, (256, many), 1)
            scores = jnp.where(at_row >= at_col, scores, -1e30)
            grown = jnp.exp(scores - jnp.max(scores, axis=-1, keepdims=True))
            total = jnp.sum(grown, axis=-1, keepdims=True)
            part = jnp.dot(grown.astype(BF16), values[0:many], preferred_element_type=F32) / total
            mixed[i, :, :, head * HD : (head + 1) * HD] = part.astype(BF16).reshape(4, TOK, HD)

    for i in range(4):
        project(i)
    share.forward()
    column.step(1)
    for i in range(4):
        attention(i)

    def rows_of(half, second):
        return mixed.at[second] if half else mixed.at[:, second]

    swaps = []
    for i, step in enumerate((1, 3, 2)):
        for half, (f, s, device) in enumerate(spots):
            cols = pl.ds(pl.multiple_of(s * 256, 256), 256)
            to = turn(s, step)
            swaps.append(
                remote(rows_of(half, to), mx.at[half, :, :, cols], mx_sends, mx_recvs, half * 3 + i, device(f, to))
            )
    keeps = []
    for half, (f, s, device) in enumerate(spots):
        cols = pl.ds(pl.multiple_of(s * 256, 256), 256)
        keeps.append(pltpu.make_async_copy(rows_of(half, s), mx.at[half, :, :, cols], local.at[half]))
        keeps[-1].start()
    share.finish()
    for copy in keeps + loads[4:]:
        copy.wait()
    for copy in swaps:
        copy.wait_recv()
    share.arrive()

    fold = Fold(spots, y, small, large, None, sends, recvs, HALF)
    for half in (0, 1):
        left = mx[half].reshape(256, 1024)
        for c in range(8):
            part = jnp.dot(left, wo[half, c].reshape(1024, 256), preferred_element_type=F32)
            y[half, :, :, c * 256 : c * 256 + 256] = part.astype(BF16).reshape(4, TOK, 256)

    fold.start(0)
    for copy in swaps:
        copy.wait_send()
    share.drain()
    fold.middle(0)
    for half in (0, 1):
        cols = slice(half * 2048, (half + 1) * 2048)
        residual[:, cols] = tokens[:, cols].astype(F32) + fold.total(half)
    moe_in[:, 0:D] = normalized(residual[...], gain[...]).astype(BF16)
    moe_in[:, D:] = extra[...]

    def block(r, half, second, start, rows):
        return everyone.at[r, half, second, pl.ds(start, rows)]

    gather = Gather(spots, block, out_sends, out_recvs, lambda half: moe_in.at[pl.ds(half * HALF, HALF)], False)
    gather.first_hop()
    keeps = []
    for half, (_, s, _) in enumerate(spots):
        keeps.append(pltpu.make_async_copy(gather.own(half), block(0, half, s, 0, HALF), local.at[half]))
        keeps[-1].start()
    fold.drain()
    gather.second_hop()
    gather.forward(0)
    column.step(2)
    gather.last_hop()
    gather.forward(1)
    gather.forward(2)
    column.step(3)
    gather.forward(3)
    for r in range(4):
        gather.finish(r)
    column.step(4)
    gather.drain()
    for keep in keeps:
        keep.wait()
    column.finish()
    own_down.wait()


def experts(
    everyone, weights, down_all, residual,
    out,
    g, w, wd, act, y, small, large, z, sends, recvs, load_g, load_w, load_down,
):
    spots = place()
    rows_of = [pltpu.make_async_copy(everyone.at[r], g.at[r], load_g.at[r]) for r in range(4)]
    feeds = []
    for c in range(6):
        part = (c // 2 + c % 2 * 3) * 256
        view = pl.ds(part, 256)
        feeds.append(pltpu.make_async_copy(weights.at[:, view], w.at[:, view], load_w.at[c]))
    downs = pltpu.make_async_copy(down_all, wd, load_down)
    rows_of[3].start()
    for copy in feeds:
        copy.start()
    downs.start()
    for r in (2, 1, 0):
        rows_of[r].start()
    meet(around(spots))
    scatter = Scatter(spots, y, small, large, z, sends, recvs)
    index = lax.axis_index("expert")

    def feed_part(r, c):
        cols = pl.ds(c * 256, 256)
        left = g[r, :, :, :, 0:D].reshape(256, D)
        gate = jnp.dot(left, w[:, cols].reshape(D, 256), preferred_element_type=F32)
        up = jnp.dot(left, w[:, pl.ds(FF + c * 256, 256)].reshape(D, 256), preferred_element_type=F32)
        act[:, cols] = (gate / (1.0 + jnp.exp(-gate)) * up).astype(BF16)

    def feed(r):
        rows_of[r].wait()
        for c in range(3):
            if r == 3:
                feeds[2 * c].wait()
                feeds[2 * c + 1].wait()
            feed_part(r, c)

    def down(r):
        table = g[r, :, :, :, D:].reshape(256, EXTRA).astype(F32)
        lanes = lax.broadcasted_iota(jnp.int32, (256, EXTRA), 1)
        chosen = (lanes == index) | (lanes == index + 16)
        share = jnp.sum(jnp.where(chosen, table, 0.0), axis=-1, keepdims=True)

        for n in range(16):
            right = wd[:, n * 48 : n * 48 + 48].reshape(FF, 256)
            part = jnp.dot(act[...], right, preferred_element_type=F32) * share
            y[r, :, :, :, n * 256 : n * 256 + 256] = part.astype(BF16).reshape(2, 4, HALF, 256)

    feed(3)
    downs.wait()
    down(3)
    scatter.start(3)
    feed(2)
    down(2)
    scatter.start(2)
    scatter.middle(3)
    feed(1)
    down(1)
    scatter.start(1)
    scatter.middle(2)
    scatter.finish(3)
    scatter.start(4)
    feed(0)
    scatter.middle(1)
    scatter.finish(2)
    down(0)
    scatter.start(0)
    scatter.finish(1)
    scatter.middle(4)
    scatter.middle(0)
    scatter.finish(0)
    for half in (0, 1):
        rows = slice(half * HALF, (half + 1) * HALF)
        out[rows] = (residual[rows] + scatter.total(half)).astype(BF16)
    scatter.drain()


def rope_tables():
    frequency = np.exp(np.arange(HD // 2, dtype=np.float32) * np.float32(-2.0 * math.log(1000000.0) / HD))
    angles = (np.arange(SEQ, dtype=np.float32)[:, None] * frequency[None, :]).astype(np.float32)
    cosine, sine = np.cos(angles), np.sin(angles)
    return (
        np.concatenate([cosine, cosine], axis=1).astype(np.float32),
        np.concatenate([-sine, sine], axis=1).astype(np.float32),
    )


VMEM = pl.BlockSpec(memory_space=pltpu.VMEM)
ANY = pl.BlockSpec(memory_space=pl.ANY)
HBM = pl.BlockSpec(memory_space=pltpu.HBM)
SEMS = pltpu.SemaphoreType.DMA((40,))
RING = [
    pltpu.VMEM((4, 2, 4, HALF, D), BF16),
    pltpu.VMEM((2, 5, 2, 16, D), BF16),
    pltpu.VMEM((2, 5, 2, HALF, D), BF16),
    pltpu.VMEM((2, 4, HALF, D), BF16),
]


def params(number, mib):
    return pltpu.CompilerParams(collective_id=number, has_side_effects=True, vmem_limit_bytes=mib * MIB)


def cost(flops, moved):
    return pl.CostEstimate(flops=flops, bytes_accessed=moved, transcendentals=0)


def local(
    tokens,
    attn_gain,
    moe_gain,
    w_query,
    w_key,
    w_value,
    w_out,
    expert_gate,
    expert_up,
    expert_down,
    routes,
    route_weights,
):
    rows = tokens[0]
    attn_shard, moe_shard, down_shard = pl.pallas_call(
        pack_kernel,
        out_shape=(
            jax.ShapeDtypeStruct((768, 256), BF16),
            jax.ShapeDtypeStruct((1536, 256), BF16),
            jax.ShapeDtypeStruct((768, 256), BF16),
        ),
        in_specs=[VMEM] * 7,
        out_specs=(VMEM, VMEM, VMEM),
        compiler_params=pltpu.CompilerParams(vmem_limit_bytes=60 * MIB),
        cost_estimate=cost(1 << 10, 4 * MIB),
        name="pack_weights",
    )(expert_gate[0], expert_up[0], expert_down[0], w_query, w_key, w_value, w_out)
    attn_weights = lax.all_gather(attn_shard, "dp", axis=0)
    moe_weights = lax.all_gather(moe_shard, "dp", axis=0)

    gathered, extra = pl.pallas_call(
        gather_kernel,
        out_shape=(jax.ShapeDtypeStruct((16, TOK, D), BF16), jax.ShapeDtypeStruct((TOK, EXTRA), BF16)),
        in_specs=[VMEM] * 4,
        out_specs=(HBM, VMEM),
        scratch_shapes=[pltpu.VMEM((TOK, D), BF16), SEMS, SEMS, pltpu.SemaphoreType.DMA],
        compiler_params=params(0, 60),
        cost_estimate=cost(1 << 10, MIB),
        name="gather_tokens",
    )(rows, attn_gain[None], routes[0].T, route_weights[0].T)

    cosine, sine = rope_tables()
    residual, everyone, down_all = pl.pallas_call(
        attend,
        out_shape=(
            jax.ShapeDtypeStruct((TOK, D), F32),
            jax.ShapeDtypeStruct((4, 2, 4, HALF, D + EXTRA), BF16),
            jax.ShapeDtypeStruct((16, 768, 256), BF16),
        ),
        in_specs=[ANY, ANY, VMEM, VMEM, VMEM, VMEM, VMEM, ANY],
        out_specs=(VMEM, HBM, HBM),
        scratch_shapes=[
            pltpu.VMEM((16, TOK, D), BF16),
            pltpu.VMEM((16, 512, 256), BF16),
            pltpu.VMEM((2, 8, 4, 256, 256), BF16),
            pltpu.VMEM((2, SEQ, HD), BF16),
            pltpu.VMEM((SEQ, HD), BF16),
            pltpu.VMEM((SEQ, HD), BF16),
            pltpu.VMEM((4, 4, TOK, 256), BF16),
            pltpu.VMEM((2, 4, TOK, 1024), BF16),
            pltpu.VMEM((TOK, D + EXTRA), BF16),
            pltpu.VMEM((2, 4, TOK, 2048), BF16),
            pltpu.VMEM((2, 1, 2, HALF, 2048), BF16),
            pltpu.VMEM((2, 1, 2, TOK, 2048), BF16),
            pltpu.SemaphoreType.DMA((16,)),
            pltpu.SemaphoreType.DMA((16,)),
            pltpu.SemaphoreType.DMA((6,)),
            pltpu.SemaphoreType.DMA((6,)),
            SEMS,
            SEMS,
            SEMS,
            SEMS,
            pltpu.SemaphoreType.DMA((17,)),
            pltpu.SemaphoreType.DMA((17,)),
            pltpu.SemaphoreType.DMA((8,)),
        ],
        compiler_params=params(1, 56),
        cost_estimate=cost(1 << 10, MIB),
        name="attention",
    )(gathered, attn_weights, rows, cosine, sine, moe_gain[None], extra, down_shard)

    layer_out = pl.pallas_call(
        experts,
        out_shape=jax.ShapeDtypeStruct((TOK, D), BF16),
        in_specs=[ANY, ANY, ANY, VMEM],
        out_specs=VMEM,
        scratch_shapes=[
            pltpu.VMEM((4, 2, 4, HALF, D + EXTRA), BF16),
            pltpu.VMEM((16, 1536, 256), BF16),
            pltpu.VMEM((16, 768, 256), BF16),
            pltpu.VMEM((256, FF), BF16),
            *RING,
            SEMS,
            SEMS,
            pltpu.SemaphoreType.DMA((4,)),
            pltpu.SemaphoreType.DMA((6,)),
            pltpu.SemaphoreType.DMA,
        ],
        compiler_params=params(2, 60),
        cost_estimate=cost(20 << 30, 200 * MIB),
        name="experts",
    )(everyone, moe_weights, down_all, residual)
    return layer_out[None]


def solution(mesh):
    return jax.shard_map(
        local,
        mesh=mesh,
        in_specs=(
            P("dp", "expert", None),
            P(),
            P(),
            P("dp", "expert"),
            P("dp", None),
            P("dp", None),
            P("expert", "dp"),
            P("expert", "dp", None),
            P("expert", "dp", None),
            P("expert", "dp", None),
            P("dp", "expert", None),
            P("dp", "expert", None),
        ),
        out_specs=P("dp", "expert", None),
        check_vma=False,
    )
```

```python
import functools
import math

import jax
import jax.numpy as jnp
import numpy as np
from jax import lax
from jax.experimental import pallas as pl
from jax.experimental.pallas import tpu as pltpu
from jax.sharding import PartitionSpec as P

HD = 128
D = 4096
FF = 768
TOK = 64
HALF = 32
SEQ = 1024
EXTRA = 128
EARLY = 1056
LATE = 480
MESH = pl.DeviceIdType.MESH
F32 = jnp.float32
BF16 = jnp.bfloat16
MIB = 1 << 20

STEP = (0, 3, 1, 2)


def place():
    index = lax.axis_index("expert")
    x, y = index // 4, index % 4
    return (
        (x, y, lambda first, second: {"expert": first * 4 + second}),
        (y, x, lambda first, second: {"expert": second * 4 + first}),
    )


def turn(coordinate, step):
    return (coordinate + step) % 4


def around(spots):
    return [device(turn(f, step), s) for f, s, device in spots for step in (1, 3)]


def meet(devices):
    barrier = pltpu.get_barrier_semaphore()
    for device in devices:
        pl.semaphore_signal(barrier, inc=1, device_id=device, device_id_type=MESH)
    pl.semaphore_wait(barrier, len(devices))


def remote(source, target, sends, recvs, slot, device):
    copy = pltpu.make_async_remote_copy(
        src_ref=source,
        dst_ref=target,
        send_sem=sends.at[slot],
        recv_sem=recvs.at[slot],
        device_id=device,
        device_id_type=MESH,
    )
    copy.start()
    return copy


class Gather:
    def __init__(self, spots, block, sends, recvs, own, absolute):
        self.spots, self.block, self.sends, self.recvs = spots, block, sends, recvs
        self.own, self.absolute = own, absolute
        self.copies = {}

    def send(self, half, group, lane, source, target, device):
        slot = (half * 5 + group) * 4 + lane
        self.copies[half, group, lane] = remote(
            source, target, self.sends, self.recvs, slot, device
        )

    def first_hop(self):
        for half, (f, s, device) in enumerate(self.spots):
            for lane, step in ((0, 1), (1, 3)):
                target = self.block(0 if self.absolute else 1 + lane, half, s, 0, HALF)
                self.send(half, 4, lane, self.own(half), target, device(turn(f, step), s))
        self.spread(0)

    def spread(self, r, halves=(0, 1)):
        for half in halves:
            f, s, device = self.spots[half]
            mine = self.own(half) if r == 0 else self.block(r, half, s, 0, HALF)
            for lane, step in ((0, 1), (1, 3)):
                self.send(half, r, lane, mine, self.block(r, half, s, 0, HALF), device(f, turn(s, step)))

    def second_hop(self):
        for lane, step in ((0, 1), (1, 3)):
            for half, (f, s, device) in enumerate(self.spots):
                self.copies[half, 4, lane].wait_recv()
                source = self.block(1 + lane, half, s, lane * 16, 16)
                target = source if self.absolute else self.block(3, half, s, lane * 16, 16)
                self.send(half, 4, 2 + lane, source, target, device(turn(f, step), s))

    def last_hop(self):
        for half in (0, 1):
            for lane in (2, 3):
                self.copies[half, 4, lane].wait_recv()
            self.spread(3, (half,))

    def forward(self, r):
        for lane, step in ((0, 1), (1, 3)):
            for half, (f, s, device) in enumerate(self.spots):
                self.copies[half, r, lane].wait_recv()
                here = self.block(r, half, turn(s, 4 - step), lane * 16, 16)
                self.send(half, r, 2 + lane, here, here, device(f, turn(s, step)))

    def finish(self, r):
        for half in (0, 1):
            for lane in (2, 3):
                self.copies[half, r, lane].wait_recv()

    def rest(self, between):
        self.second_hop()
        self.forward(0)
        self.spread(1)
        self.last_hop()
        self.spread(2)
        between[0]()
        self.forward(1)
        between[1]()
        self.forward(3)
        self.forward(2)
        between[2]()
        for r in range(4):
            self.finish(r)
        between[3]()
        self.drain()

    def drain(self):
        for copy in self.copies.values():
            copy.wait_send()


class Scatter:
    def __init__(self, spots, y_ref, small, large, z_ref, sends, recvs, cut=HALF // 2):
        self.spots, self.y, self.small, self.large, self.z = spots, y_ref, small, large, z_ref
        self.sends, self.recvs, self.cut = sends, recvs, cut
        self.copies = {}

    def send(self, half, group, lane, source, target, device):
        slot = (half * 5 + group) * 4 + lane
        self.copies[half, group, lane] = remote(
            source, target, self.sends, self.recvs, slot, device
        )

    def parts(self, half, group):
        f, s, device = self.spots[half]
        if group < 4:
            return (
                lambda step: self.y.at[group, half, turn(s, step)],
                lambda step: device(f, turn(s, step)),
            )
        return (
            lambda step: self.z.at[half, STEP.index(step)],
            lambda step: device(turn(f, step), s),
        )

    def start(self, group, halves=(0, 1)):
        for half in halves:
            block, device = self.parts(half, group)
            for lane, step in ((0, 1), (1, 3)):
                self.send(
                    half, group, lane, block(2).at[pl.ds(lane * self.cut, self.cut)], self.small.at[half, group, lane],
                    device(step),
                )

    def middle(self, group):
        for lane, step in ((0, 1), (1, 3)):
            for half in (0, 1):
                block, device = self.parts(half, group)
                self.copies[half, group, lane].wait_recv()
                rows = block(step).at[pl.ds(lane * self.cut, self.cut)]
                rows[...] = (rows[...].astype(F32) + self.small[half, group, lane].astype(F32)).astype(BF16)
                self.send(half, group, 2 + lane, block(step), self.large.at[half, group, lane], device(step))

    def arrived(self, half, group):
        for lane in (2, 3):
            self.copies[half, group, lane].wait_recv()
        return self.large[half, group, 0].astype(F32) + self.large[half, group, 1].astype(F32)

    def finish(self, group):
        for half in (0, 1):
            _, s, _ = self.spots[half]
            total = self.arrived(half, group) + self.y[group, half, s].astype(F32)
            self.z[half, group] = total.astype(BF16)

    def total(self, half):
        return self.arrived(half, 4) + self.z[half, 0].astype(F32)

    def drain(self):
        for copy in self.copies.values():
            copy.wait_send()


class Fold(Scatter):
    def parts(self, half, group):
        f, s, device = self.spots[half]
        return (lambda step: self.y.at[half, turn(f, step)], lambda step: device(turn(f, step), s))

    def total(self, half):
        return self.arrived(half, 0) + self.y[half, self.spots[half][0]].astype(F32)


class Column:
    def __init__(self, mine, w_ref, rows, sends, recvs):
        index = lax.axis_index("dp")
        self.mine, self.w, self.rows, self.sends, self.recvs = mine, w_ref, rows, sends, recvs
        self.level, self.core = index // 2, index % 2
        self.other = {"dp": self.level * 2 + 1 - self.core}
        self.next = [{"dp": (self.level + step) % 8 * 2 + self.core} for step in (1, 7)]
        self.copies = {}

    def send(self, slot, step, device, way=None):
        start, rows = (0, self.rows) if way is None else (way * self.rows // 2, self.rows // 2)
        place = self.w.at[(self.level + step) % 8 * 2 + self.core, pl.ds(start, rows)]
        source = place if step else self.mine
        self.copies[slot] = remote(source, place, self.sends, self.recvs, slot, device)

    def start(self):
        for way in (0, 1):
            self.send(way * 4, 0, self.next[way])
        self.send(8, 0, self.other)

    def step(self, t):
        for way in (0, 1):
            self.copies[way * 4 + t - 1].wait_recv()
            here = t if way else 8 - t
            if t < 4:
                self.send(way * 4 + t, here, self.next[way], way if t == 3 else None)
            self.send(8 + way * 4 + t, here, self.other, way if t == 4 else None)

    def finish(self):
        for slot in range(8, 17):
            self.copies[slot].wait_recv()
        for copy in self.copies.values():
            copy.wait_send()


def normalized(values, gain):
    return values * lax.rsqrt(jnp.mean(values * values, axis=-1, keepdims=True) + 1e-06) * gain


def gather_kernel(
    tokens, gain, routes, weights, gate, up, down, w_query, w_key, w_value, w_out,
    out, extra, w_all, feed_shard, down_shard,
    own, parts, wide, tall, shard, sends, recvs, w_sends, w_recvs, local,
):
    spots = place()
    index = lax.axis_index("expert")
    loads = [
        pltpu.make_async_copy(source, target, local.at[i])
        for i, (source, target) in enumerate(
            (
                (w_query, parts.at[0]),
                (w_key, parts.at[1]),
                (w_value, parts.at[2]),
                (w_out, parts.at[3]),
                (down, tall),
                (gate, wide.at[0]),
                (up, wide.at[1]),
            )
        )
    ]
    for copy in loads:
        copy.start()
    own[...] = normalized(tokens[...].astype(F32), gain[...]).astype(BF16)
    keep = pltpu.make_async_copy(own, out.at[index], local.at[7])
    keep.start()
    column = Column(shard, w_all, EARLY, w_sends, w_recvs)
    meet(around(spots) + column.next + [column.other])

    def block(r, half, second, start, rows):
        f, _, device = spots[half]
        return out.at[device(turn(f, STEP[r]), second)["expert"], pl.ds(half * HALF + start, rows)]

    gather = Gather(spots, block, sends, recvs, lambda half: own.at[pl.ds(half * HALF, HALF)], True)
    gather.first_hop()

    for copy in loads:
        copy.wait()
    key_cols = pl.ds(pl.multiple_of(index // 8 * HD, HD), HD)
    shard[0:256] = parts[0]
    shard[256:512, 0:HD] = parts[1, :, key_cols]
    shard[256:512, HD:] = parts[2, :, key_cols]
    shard[512:768] = parts[3]
    for c in range(6):
        shard[768 + c * 48 : 816 + c * 48] = tall[:, c * 256 : c * 256 + 256]
    mine = pltpu.make_async_copy(shard, w_all.at[lax.axis_index("dp")], local.at[0])
    mine.start()
    column.start()
    for c in range(6, 16):
        down_shard[c * 48 - 288 : c * 48 - 240] = tall[:, c * 256 : c * 256 + 256]
    for c in range(6):
        feed_shard[c * 256 : c * 256 + 256] = wide[c // 3, :, c % 3 * 256 : c % 3 * 256 + 256]

    share = weights[...] / jnp.sum(weights[...], axis=0, keepdims=True)
    high = share.astype(BF16).astype(F32)
    low = share - high
    at_row = lax.broadcasted_iota(jnp.int32, (EXTRA, TOK), 0)
    table = jnp.zeros((EXTRA, TOK), F32)
    for k in range(routes.shape[0]):
        named = routes[k : k + 1]
        table += jnp.where(at_row == named, high[k : k + 1], 0.0)
        table += jnp.where(at_row == named + 16, low[k : k + 1], 0.0)
    extra[...] = table.T.astype(BF16)

    gather.rest([lambda t=t: column.step(t) for t in (1, 2, 3, 4)])
    keep.wait()
    mine.wait()
    column.finish()


class Share:
    def __init__(self, spots, weights, wo, sends, recvs):
        index = lax.axis_index("dp")
        self.core = index % 2
        self.other = {"dp": index + 1 - 2 * self.core}
        self.spots, self.weights, self.wo, self.sends, self.recvs = spots, weights, wo, sends, recvs
        self.copies = {}

    def block(self, half, second, start, count):
        return self.wo.at[half, pl.ds(4 * self.core + start, count), second]

    def send(self, half, lane, source, target, device):
        self.copies[half, lane] = remote(source, target, self.sends, self.recvs, half * 8 + lane, device)

    def start(self):
        for half, (f, s, device) in enumerate(self.spots):
            source = self.weights.at[pl.ds(8 * half + 4 * self.core, 4), pl.ds(512, 256)]
            for lane, step in ((0, 1), (1, 3)):
                self.send(half, lane, source, self.block(half, s, 0, 4), device(f, turn(s, step)))

    def forward(self):
        for lane, step in ((0, 1), (1, 3)):
            for half, (f, s, device) in enumerate(self.spots):
                self.copies[half, lane].wait_recv()
                here = self.block(half, turn(s, 4 - step), 2 * lane, 2)
                self.send(half, 2 + lane, here, here, device(f, turn(s, step)))
                here = self.block(half, turn(s, 4 - step), 0, 4)
                self.send(half, 4 + lane, here, here, self.other)

    def finish(self):
        for lane in (0, 1):
            for half, (f, s, device) in enumerate(self.spots):
                self.copies[half, 2 + lane].wait_recv()
                here = self.block(half, turn(s, 2), 2 * lane, 2)
                self.send(half, 6 + lane, here, here, self.other)

    def arrive(self):
        for half in (0, 1):
            for lane in range(4, 8):
                self.copies[half, lane].wait_recv()

    def drain(self):
        for copy in self.copies.values():
            copy.wait_send()


def attend(
    gathered, weights, tokens, cosine, sine, gain, extra, down_shard,
    residual, everyone, down_all,
    x, w, wo, queries, keys, values, mixed, mx, moe_in, y, small, large,
    wo_sends, wo_recvs, mx_sends, mx_recvs, sends, recvs, out_sends, out_recvs, z_sends, z_recvs, local,
):
    spots = place()
    load_w = pltpu.make_async_copy(weights.at[:, pl.ds(0, 512)], w, local.at[0])
    load_w.start()
    loads = []
    for i in range(4):
        loads.append(pltpu.make_async_copy(gathered.at[pl.ds(i * 4, 4)], x.at[pl.ds(i * 4, 4)], local.at[1 + i]))
        loads[-1].start()
    for half, (f, s, _) in enumerate(spots):
        loads.append(
            pltpu.make_async_copy(
                weights.at[pl.ds(8 * half, 8), pl.ds(512, 256)], wo.at[half, :, s], local.at[5 + half]
            )
        )
        loads[-1].start()
    share = Share(spots, weights, wo, wo_sends, wo_recvs)
    across = [device(f, turn(s, 2)) for f, s, device in spots]
    column = Column(down_shard, down_all, LATE, z_sends, z_recvs)
    own_down = pltpu.make_async_copy(down_shard, down_all.at[lax.axis_index("dp")], local.at[7])
    own_down.start()
    meet(around(spots) + across + column.next + [column.other])
    share.start()
    column.start()
    load_w.wait()

    def rope(part, rows):
        return part * cosine[rows] + pltpu.roll(part, HD // 2, 1) * sine[rows]

    def project(i):
        loads[i].wait()
        rows = slice(i * 256, i * 256 + 256)
        left = x[i * 4 : i * 4 + 4].reshape(256, D)
        q = jnp.dot(left, w[:, 0:256].reshape(D, 256), preferred_element_type=F32)
        for head in (0, 1):
            queries[head, rows] = rope(q[:, head * HD : (head + 1) * HD], rows).astype(BF16)
        kv = jnp.dot(left, w[:, 256:512].reshape(D, 256), preferred_element_type=F32)
        keys[rows] = rope(kv[:, :HD], rows).astype(BF16)
        values[rows] = kv[:, HD:].astype(BF16)

    def attention(i):
        many = (i + 1) * 256
        for head in (0, 1):
            scores = lax.dot_general(
                queries[head, i * 256 : many], keys[0:many], (((1,), (1,)), ((), ())), preferred_element_type=F32
            ) * (1.0 / math.sqrt(HD))
            at_row = lax.broadcasted_iota(jnp.int32, (256, many), 0) + i * 256
            at_col = lax.broadcasted_iota(jnp.int32, (256, many), 1)
            scores = jnp.where(at_row >= at_col, scores, -1e30)
            grown = jnp.exp(scores - jnp.max(scores, axis=-1, keepdims=True))
            total = jnp.sum(grown, axis=-1, keepdims=True)
            part = jnp.dot(grown.astype(BF16), values[0:many], preferred_element_type=F32) / total
            mixed[i, :, :, head * HD : (head + 1) * HD] = part.astype(BF16).reshape(4, TOK, HD)

    for i in range(4):
        project(i)
    share.forward()
    column.step(1)
    for i in range(4):
        attention(i)

    def rows_of(half, second):
        return mixed.at[second] if half else mixed.at[:, second]

    swaps = []
    for i, step in enumerate((1, 3, 2)):
        for half, (f, s, device) in enumerate(spots):
            cols = pl.ds(pl.multiple_of(s * 256, 256), 256)
            to = turn(s, step)
            swaps.append(
                remote(rows_of(half, to), mx.at[half, :, :, cols], mx_sends, mx_recvs, half * 3 + i, device(f, to))
            )
    keeps = []
    for half, (f, s, device) in enumerate(spots):
        cols = pl.ds(pl.multiple_of(s * 256, 256), 256)
        keeps.append(pltpu.make_async_copy(rows_of(half, s), mx.at[half, :, :, cols], local.at[half]))
        keeps[-1].start()
    share.finish()
    for copy in keeps + loads[4:]:
        copy.wait()
    for copy in swaps:
        copy.wait_recv()
    share.arrive()

    fold = Fold(spots, y, small, large, None, sends, recvs, HALF)
    for half in (0, 1):
        left = mx[half].reshape(256, 1024)
        for c in range(8):
            part = jnp.dot(left, wo[half, c].reshape(1024, 256), preferred_element_type=F32)
            y[half, :, :, c * 256 : c * 256 + 256] = part.astype(BF16).reshape(4, TOK, 256)
        fold.start(0, (half,))
    for copy in swaps:
        copy.wait_send()
    share.drain()
    column.step(2)
    fold.middle(0)
    for half in (0, 1):
        cols = slice(half * 2048, (half + 1) * 2048)
        residual[:, cols] = tokens[:, cols].astype(F32) + fold.total(half)
    moe_in[:, 0:D] = normalized(residual[...], gain[...]).astype(BF16)
    moe_in[:, D:] = extra[...]

    def block(r, half, second, start, rows):
        return everyone.at[r, half, second, pl.ds(start, rows)]

    gather = Gather(spots, block, out_sends, out_recvs, lambda half: moe_in.at[pl.ds(half * HALF, HALF)], False)
    gather.first_hop()
    keeps = []
    for half, (_, s, _) in enumerate(spots):
        keeps.append(pltpu.make_async_copy(gather.own(half), block(0, half, s, 0, HALF), local.at[half]))
        keeps[-1].start()
    fold.drain()
    gather.rest([lambda: column.step(3), lambda: column.step(4), lambda: None, lambda: None])
    for keep in keeps:
        keep.wait()
    column.finish()
    own_down.wait()


def experts(
    everyone, weights, w_all, down_all, residual,
    out,
    g, w, wd, act, y, small, large, z, sends, recvs, load_g, load_w, load_down,
):
    spots = place()
    rows_of = [pltpu.make_async_copy(everyone.at[r], g.at[r], load_g.at[r]) for r in range(4)]
    feeds = []
    for c in range(6):
        part = (c // 2 + c % 2 * 3) * 256
        view = pl.ds(part, 256)
        feeds.append(pltpu.make_async_copy(weights.at[:, view], w.at[:, view], load_w.at[c]))
    downs = [
        pltpu.make_async_copy(w_all.at[:, pl.ds(768, 288)], wd.at[:, pl.ds(0, 288)], load_down.at[0]),
        pltpu.make_async_copy(down_all, wd.at[:, pl.ds(288, LATE)], load_down.at[1]),
    ]
    rows_of[3].start()
    for copy in feeds:
        copy.start()
    for copy in downs:
        copy.start()
    for r in (2, 1, 0):
        rows_of[r].start()
    meet(around(spots))
    scatter = Scatter(spots, y, small, large, z, sends, recvs)
    index = lax.axis_index("expert")

    def feed_part(r, c):
        cols = pl.ds(c * 256, 256)
        left = g[r, :, :, :, 0:D].reshape(256, D)
        gate = jnp.dot(left, w[:, cols].reshape(D, 256), preferred_element_type=F32)
        up = jnp.dot(left, w[:, pl.ds(FF + c * 256, 256)].reshape(D, 256), preferred_element_type=F32)
        act[:, cols] = (gate / (1.0 + jnp.exp(-gate)) * up).astype(BF16)

    def feed(r):
        rows_of[r].wait()
        for c in range(3):
            if r == 3:
                feeds[2 * c].wait()
                feeds[2 * c + 1].wait()
            feed_part(r, c)

    def down(r):
        table = g[r, :, :, :, D:].reshape(256, EXTRA).astype(F32)
        lanes = lax.broadcasted_iota(jnp.int32, (256, EXTRA), 1)
        chosen = (lanes == index) | (lanes == index + 16)
        share = jnp.sum(jnp.where(chosen, table, 0.0), axis=-1, keepdims=True)

        for n in range(16):
            right = wd[:, n * 48 : n * 48 + 48].reshape(FF, 256)
            part = jnp.dot(act[...], right, preferred_element_type=F32) * share
            y[r, :, :, :, n * 256 : n * 256 + 256] = part.astype(BF16).reshape(2, 4, HALF, 256)

    feed(3)
    for copy in downs:
        copy.wait()
    down(3)
    scatter.start(3)
    feed(2)
    down(2)
    scatter.start(2)
    scatter.middle(3)
    feed(1)
    down(1)
    scatter.start(1)
    scatter.middle(2)
    scatter.finish(3)
    scatter.start(4)
    feed(0)
    scatter.middle(1)
    scatter.finish(2)
    down(0)
    scatter.start(0)
    scatter.finish(1)
    scatter.middle(4)
    scatter.middle(0)
    scatter.finish(0)
    for half in (0, 1):
        rows = slice(half * HALF, (half + 1) * HALF)
        out[rows] = (residual[rows] + scatter.total(half)).astype(BF16)
    scatter.drain()


def rope_tables():
    frequency = np.exp(np.arange(HD // 2, dtype=np.float32) * np.float32(-2.0 * math.log(1000000.0) / HD))
    angles = (np.arange(SEQ, dtype=np.float32)[:, None] * frequency[None, :]).astype(np.float32)
    cosine, sine = np.cos(angles), np.sin(angles)
    return (
        np.concatenate([cosine, cosine], axis=1).astype(np.float32),
        np.concatenate([-sine, sine], axis=1).astype(np.float32),
    )


VMEM = pl.BlockSpec(memory_space=pltpu.VMEM)
ANY = pl.BlockSpec(memory_space=pl.ANY)
HBM = pl.BlockSpec(memory_space=pltpu.HBM)
SEMS = pltpu.SemaphoreType.DMA((40,))
RING = [
    pltpu.VMEM((4, 2, 4, HALF, D), BF16),
    pltpu.VMEM((2, 5, 2, 16, D), BF16),
    pltpu.VMEM((2, 5, 2, HALF, D), BF16),
    pltpu.VMEM((2, 4, HALF, D), BF16),
]


def params(number, mib):
    return pltpu.CompilerParams(collective_id=number, has_side_effects=True, vmem_limit_bytes=mib * MIB)


def cost(flops, moved):
    return pl.CostEstimate(flops=flops, bytes_accessed=moved, transcendentals=0)


def local(
    tokens,
    attn_gain,
    moe_gain,
    w_query,
    w_key,
    w_value,
    w_out,
    expert_gate,
    expert_up,
    expert_down,
    routes,
    route_weights,
):
    rows = tokens[0]
    gathered, extra, w_all, feed_shard, down_shard = pl.pallas_call(
        gather_kernel,
        out_shape=(
            jax.ShapeDtypeStruct((16, TOK, D), BF16),
            jax.ShapeDtypeStruct((TOK, EXTRA), BF16),
            jax.ShapeDtypeStruct((16, EARLY, 256), BF16),
            jax.ShapeDtypeStruct((1536, 256), BF16),
            jax.ShapeDtypeStruct((LATE, 256), BF16),
        ),
        in_specs=[VMEM] * 4 + [ANY] * 7,
        out_specs=(HBM, VMEM, HBM, VMEM, VMEM),
        scratch_shapes=[
            pltpu.VMEM((TOK, D), BF16),
            pltpu.VMEM((4, 256, 256), BF16),
            pltpu.VMEM((2, 256, FF), BF16),
            pltpu.VMEM((48, D), BF16),
            pltpu.VMEM((EARLY, 256), BF16),
            SEMS,
            SEMS,
            pltpu.SemaphoreType.DMA((17,)),
            pltpu.SemaphoreType.DMA((17,)),
            pltpu.SemaphoreType.DMA((8,)),
        ],
        compiler_params=params(0, 60),
        cost_estimate=cost(1 << 10, MIB),
        name="gather_tokens",
    )(
        rows, attn_gain[None], routes[0].T, route_weights[0].T,
        expert_gate[0], expert_up[0], expert_down[0], w_query, w_key, w_value, w_out,
    )
    feed_weights = lax.all_gather(feed_shard, "dp", axis=0)

    cosine, sine = rope_tables()
    residual, everyone, down_all = pl.pallas_call(
        attend,
        out_shape=(
            jax.ShapeDtypeStruct((TOK, D), F32),
            jax.ShapeDtypeStruct((4, 2, 4, HALF, D + EXTRA), BF16),
            jax.ShapeDtypeStruct((16, LATE, 256), BF16),
        ),
        in_specs=[ANY, ANY, VMEM, VMEM, VMEM, VMEM, VMEM, ANY],
        out_specs=(VMEM, HBM, HBM),
        scratch_shapes=[
            pltpu.VMEM((16, TOK, D), BF16),
            pltpu.VMEM((16, 512, 256), BF16),
            pltpu.VMEM((2, 8, 4, 256, 256), BF16),
            pltpu.VMEM((2, SEQ, HD), BF16),
            pltpu.VMEM((SEQ, HD), BF16),
            pltpu.VMEM((SEQ, HD), BF16),
            pltpu.VMEM((4, 4, TOK, 256), BF16),
            pltpu.VMEM((2, 4, TOK, 1024), BF16),
            pltpu.VMEM((TOK, D + EXTRA), BF16),
            pltpu.VMEM((2, 4, TOK, 2048), BF16),
            pltpu.VMEM((2, 1, 2, HALF, 2048), BF16),
            pltpu.VMEM((2, 1, 2, TOK, 2048), BF16),
            pltpu.SemaphoreType.DMA((16,)),
            pltpu.SemaphoreType.DMA((16,)),
            pltpu.SemaphoreType.DMA((6,)),
            pltpu.SemaphoreType.DMA((6,)),
            SEMS,
            SEMS,
            SEMS,
            SEMS,
            pltpu.SemaphoreType.DMA((17,)),
            pltpu.SemaphoreType.DMA((17,)),
            pltpu.SemaphoreType.DMA((8,)),
        ],
        compiler_params=params(1, 56),
        cost_estimate=cost(1 << 10, MIB),
        name="attention",
    )(gathered, w_all, rows, cosine, sine, moe_gain[None], extra, down_shard)

    layer_out = pl.pallas_call(
        experts,
        out_shape=jax.ShapeDtypeStruct((TOK, D), BF16),
        in_specs=[ANY, ANY, ANY, ANY, VMEM],
        out_specs=VMEM,
        scratch_shapes=[
            pltpu.VMEM((4, 2, 4, HALF, D + EXTRA), BF16),
            pltpu.VMEM((16, 1536, 256), BF16),
            pltpu.VMEM((16, 768, 256), BF16),
            pltpu.VMEM((256, FF), BF16),
            *RING,
            SEMS,
            SEMS,
            pltpu.SemaphoreType.DMA((4,)),
            pltpu.SemaphoreType.DMA((6,)),
            pltpu.SemaphoreType.DMA((2,)),
        ],
        compiler_params=params(2, 60),
        cost_estimate=cost(20 << 30, 200 * MIB),
        name="experts",
    )(everyone, feed_weights, w_all, down_all, residual)
    return layer_out[None]


def solution(mesh):
    return jax.shard_map(
        local,
        mesh=mesh,
        in_specs=(
            P("dp", "expert", None),
            P(),
            P(),
            P("dp", "expert"),
            P("dp", None),
            P("dp", None),
            P("expert", "dp"),
            P("expert", "dp", None),
            P("expert", "dp", None),
            P("expert", "dp", None),
            P("dp", "expert", None),
            P("dp", "expert", None),
        ),
        out_specs=P("dp", "expert", None),
        check_vma=False,
    )
```

```python
import functools
import math

import jax
import jax.numpy as jnp
import numpy as np
from jax import lax
from jax.experimental import pallas as pl
from jax.experimental.pallas import tpu as pltpu
from jax.sharding import PartitionSpec as P

HD = 128
D = 4096
FF = 768
TOK = 64
HALF = 32
SEQ = 1024
EXTRA = 128
EARLY = ((0, 512), (512, 256))
LATE = ((0, 576), (576, 576), (1152, 576), (1728, 576))
MESH = pl.DeviceIdType.MESH
F32 = jnp.float32
BF16 = jnp.bfloat16
MIB = 1 << 20

STEP = (0, 3, 1, 2)


def place():
    index = lax.axis_index("expert")
    x, y = index // 4, index % 4
    return (
        (x, y, lambda first, second: {"expert": first * 4 + second}),
        (y, x, lambda first, second: {"expert": second * 4 + first}),
    )


def turn(coordinate, step):
    return (coordinate + step) % 4


def around(spots):
    return [device(turn(f, step), s) for f, s, device in spots for step in (1, 3)]


def meet(devices):
    barrier = pltpu.get_barrier_semaphore()
    for device in devices:
        pl.semaphore_signal(barrier, inc=1, device_id=device, device_id_type=MESH)
    pl.semaphore_wait(barrier, len(devices))


def remote(source, target, sends, recvs, slot, device):
    copy = pltpu.make_async_remote_copy(
        src_ref=source,
        dst_ref=target,
        send_sem=sends.at[slot],
        recv_sem=recvs.at[slot],
        device_id=device,
        device_id_type=MESH,
    )
    copy.start()
    return copy


class Gather:
    def __init__(self, spots, block, sends, recvs, own, absolute):
        self.spots, self.block, self.sends, self.recvs = spots, block, sends, recvs
        self.own, self.absolute = own, absolute
        self.copies = {}

    def send(self, half, group, lane, source, target, device):
        slot = (half * 5 + group) * 4 + lane
        self.copies[half, group, lane] = remote(
            source, target, self.sends, self.recvs, slot, device
        )

    def first_hop(self):
        for half, (f, s, device) in enumerate(self.spots):
            for lane, step in ((0, 1), (1, 3)):
                target = self.block(0 if self.absolute else 1 + lane, half, s, 0, HALF)
                self.send(half, 4, lane, self.own(half), target, device(turn(f, step), s))
        self.spread(0)

    def spread(self, r, halves=(0, 1)):
        for half in halves:
            f, s, device = self.spots[half]
            mine = self.own(half) if r == 0 else self.block(r, half, s, 0, HALF)
            for lane, step in ((0, 1), (1, 3)):
                self.send(half, r, lane, mine, self.block(r, half, s, 0, HALF), device(f, turn(s, step)))

    def second_hop(self):
        for lane, step in ((0, 1), (1, 3)):
            for half, (f, s, device) in enumerate(self.spots):
                self.copies[half, 4, lane].wait_recv()
                source = self.block(1 + lane, half, s, lane * 16, 16)
                target = source if self.absolute else self.block(3, half, s, lane * 16, 16)
                self.send(half, 4, 2 + lane, source, target, device(turn(f, step), s))

    def last_hop(self):
        for half in (0, 1):
            for lane in (2, 3):
                self.copies[half, 4, lane].wait_recv()
            self.spread(3, (half,))

    def forward(self, r):
        for lane, step in ((0, 1), (1, 3)):
            for half, (f, s, device) in enumerate(self.spots):
                self.copies[half, r, lane].wait_recv()
                here = self.block(r, half, turn(s, 4 - step), lane * 16, 16)
                self.send(half, r, 2 + lane, here, here, device(f, turn(s, step)))

    def finish(self, r):
        for half in (0, 1):
            for lane in (2, 3):
                self.copies[half, r, lane].wait_recv()

    def rest(self, between):
        self.second_hop()
        self.forward(0)
        between[0]()
        self.spread(1)
        self.last_hop()
        self.spread(2)
        between[1]()
        self.forward(1)
        between[2]()
        self.forward(3)
        between[3]()
        self.forward(2)
        between[4]()
        for r in range(4):
            self.finish(r)
        between[5]()
        self.drain()

    def drain(self):
        for copy in self.copies.values():
            copy.wait_send()


class Scatter:
    def __init__(self, spots, y_ref, small, large, z_ref, sends, recvs, cut=HALF // 2):
        self.spots, self.y, self.small, self.large, self.z = spots, y_ref, small, large, z_ref
        self.sends, self.recvs, self.cut = sends, recvs, cut
        self.copies = {}

    def send(self, half, group, lane, source, target, device):
        slot = (half * 5 + group) * 4 + lane
        self.copies[half, group, lane] = remote(
            source, target, self.sends, self.recvs, slot, device
        )

    def parts(self, half, group):
        f, s, device = self.spots[half]
        if group < 4:
            return (
                lambda step: self.y.at[group, half, turn(s, step)],
                lambda step: device(f, turn(s, step)),
            )
        return (
            lambda step: self.z.at[half, STEP.index(step)],
            lambda step: device(turn(f, step), s),
        )

    def start(self, group, halves=(0, 1)):
        for half in halves:
            block, device = self.parts(half, group)
            for lane, step in ((0, 1), (1, 3)):
                self.send(
                    half, group, lane, block(2).at[pl.ds(lane * self.cut, self.cut)], self.small.at[half, group, lane],
                    device(step),
                )

    def middle(self, group):
        for lane, step in ((0, 1), (1, 3)):
            for half in (0, 1):
                block, device = self.parts(half, group)
                self.copies[half, group, lane].wait_recv()
                rows = block(step).at[pl.ds(lane * self.cut, self.cut)]
                rows[...] = (rows[...].astype(F32) + self.small[half, group, lane].astype(F32)).astype(BF16)
                self.send(half, group, 2 + lane, block(step), self.large.at[half, group, lane], device(step))

    def arrived(self, half, group):
        for lane in (2, 3):
            self.copies[half, group, lane].wait_recv()
        return self.large[half, group, 0].astype(F32) + self.large[half, group, 1].astype(F32)

    def finish(self, group):
        for half in (0, 1):
            _, s, _ = self.spots[half]
            total = self.arrived(half, group) + self.y[group, half, s].astype(F32)
            self.z[half, group] = total.astype(BF16)

    def total(self, half):
        return self.arrived(half, 4) + self.z[half, 0].astype(F32)

    def drain(self):
        for copy in self.copies.values():
            copy.wait_send()


class Fold(Scatter):
    def parts(self, half, group):
        f, s, device = self.spots[half]
        return (lambda step: self.y.at[half, turn(f, step)], lambda step: device(turn(f, step), s))

    def total(self, half):
        return self.arrived(half, 0) + self.y[half, self.spots[half][0]].astype(F32)


class Column:
    def __init__(self, mine, w_ref, base, rows, sends, recvs):
        index = lax.axis_index("dp")
        self.mine, self.w, self.base, self.rows, self.sends, self.recvs = mine, w_ref, base, rows, sends, recvs
        self.level, self.core = index // 2, index % 2
        self.other = {"dp": self.level * 2 + 1 - self.core}
        self.next = [{"dp": (self.level + step) % 8 * 2 + self.core} for step in (1, 7)]
        self.copies = {}

    def send(self, slot, step, device, way=None):
        start, rows = (0, self.rows) if way is None else (way * self.rows // 2, self.rows // 2)
        place = self.w.at[(self.level + step) % 8 * 2 + self.core, pl.ds(self.base + start, rows)]
        source = place if step else self.mine
        self.copies[slot] = remote(source, place, self.sends, self.recvs, slot, device)

    def start(self):
        for way in (0, 1):
            self.send(way * 4, 0, self.next[way])
        self.send(8, 0, self.other)

    def step(self, t):
        for way in (0, 1):
            self.copies[way * 4 + t - 1].wait_recv()
            here = t if way else 8 - t
            if t < 4:
                self.send(way * 4 + t, here, self.next[way], way if t == 3 else None)
            self.send(8 + way * 4 + t, here, self.other, way if t == 4 else None)

    def finish(self):
        for slot in range(8, 17):
            self.copies[slot].wait_recv()
        for copy in self.copies.values():
            copy.wait_send()


class Columns:
    def __init__(self, mine, w_ref, parts, sends, recvs):
        self.all = [
            Column(mine.at[pl.ds(base, rows)], w_ref, base, rows, sends.at[i], recvs.at[i])
            for i, (base, rows) in enumerate(parts)
        ]
        self.near = self.all[0].next + [self.all[0].other]

    def start(self):
        for column in self.all:
            column.start()

    def steps(self, *todo, then=None):
        def run():
            for which, t in todo:
                self.all[which].step(t)
            if then:
                then()

        return run

    def finish(self):
        for column in self.all:
            column.finish()


def normalized(values, gain):
    return values * lax.rsqrt(jnp.mean(values * values, axis=-1, keepdims=True) + 1e-06) * gain


class Share:
    def __init__(self, spots, weights, wo, sends, recvs):
        index = lax.axis_index("dp")
        self.core = index % 2
        self.other = {"dp": index + 1 - 2 * self.core}
        self.spots, self.weights, self.wo, self.sends, self.recvs = spots, weights, wo, sends, recvs
        self.copies = {}

    def block(self, half, second, start, count):
        return self.wo.at[half, pl.ds(4 * self.core + start, count), second]

    def send(self, half, lane, source, target, device):
        self.copies[half, lane] = remote(source, target, self.sends, self.recvs, half * 8 + lane, device)

    def start(self):
        for half, (f, s, device) in enumerate(self.spots):
            source = self.weights.at[pl.ds(8 * half + 4 * self.core, 4), pl.ds(512, 256)]
            for lane, step in ((0, 1), (1, 3)):
                self.send(half, lane, source, self.block(half, s, 0, 4), device(f, turn(s, step)))

    def forward(self):
        for lane, step in ((0, 1), (1, 3)):
            for half, (f, s, device) in enumerate(self.spots):
                self.copies[half, lane].wait_recv()
                here = self.block(half, turn(s, 4 - step), 2 * lane, 2)
                self.send(half, 2 + lane, here, here, device(f, turn(s, step)))
                here = self.block(half, turn(s, 4 - step), 0, 4)
                self.send(half, 4 + lane, here, here, self.other)

    def finish(self):
        for lane in (0, 1):
            for half, (f, s, device) in enumerate(self.spots):
                self.copies[half, 2 + lane].wait_recv()
                here = self.block(half, turn(s, 2), 2 * lane, 2)
                self.send(half, 6 + lane, here, here, self.other)

    def arrive(self):
        for half in (0, 1):
            for lane in range(4, 8):
                self.copies[half, lane].wait_recv()

    def drain(self):
        for copy in self.copies.values():
            copy.wait_send()


def attend(
    tokens, attn_gain, moe_gain, routes, route_weights, cosine, sine,
    gate, up, down, w_query, w_key, w_value, w_out,
    residual, everyone, w_late,
    own, parts, wide, tall, shard, late_shard, x, w_all, wo, queries, keys, values, mixed, mx, moe_in, y, small, large,
    in_sends, in_recvs, w_sends, w_recvs, wo_sends, wo_recvs, mx_sends, mx_recvs, sends, recvs, out_sends, out_recvs,
    z_sends, z_recvs, local,
):
    spots = place()
    index = lax.axis_index("expert")
    loads = [
        pltpu.make_async_copy(source, target, local.at[i])
        for i, (source, target) in enumerate(
            (
                (w_query, parts.at[0]),
                (w_key, parts.at[1]),
                (w_value, parts.at[2]),
                (w_out, parts.at[3]),
                (down, tall),
                (gate, wide.at[0]),
                (up, wide.at[1]),
            )
        )
    ]
    for copy in loads:
        copy.start()
    own[...] = normalized(tokens[...].astype(F32), attn_gain[...]).astype(BF16)
    x[index] = own[...]
    early = Columns(shard, w_all, EARLY, w_sends, w_recvs)
    late = Columns(late_shard, w_late, LATE, z_sends, z_recvs)
    share_out = Share(spots, w_all, wo, wo_sends, wo_recvs)
    across = [device(f, turn(s, 2)) for f, s, device in spots]
    meet(around(spots) + across + early.near)

    def block(r, half, second, start, rows):
        f, _, device = spots[half]
        return x.at[device(turn(f, STEP[r]), second)["expert"], pl.ds(half * HALF + start, rows)]

    gather = Gather(spots, block, in_sends, in_recvs, lambda half: own.at[pl.ds(half * HALF, HALF)], True)
    gather.first_hop()

    for copy in loads:
        copy.wait()
    key_cols = pl.ds(pl.multiple_of(index // 8 * HD, HD), HD)
    shard[0:256] = parts[0]
    shard[256:512, 0:HD] = parts[1, :, key_cols]
    shard[256:512, HD:] = parts[2, :, key_cols]
    shard[512:768] = parts[3]
    w_all[lax.axis_index("dp")] = shard[...]
    early.start()
    for c in range(6):
        late_shard[c * 256 : c * 256 + 256] = wide[c // 3, :, c % 3 * 256 : c % 3 * 256 + 256]
    for c in range(16):
        late_shard[2 * FF + c * 48 : 2 * FF + c * 48 + 48] = tall[:, c * 256 : c * 256 + 256]

    own_late = pltpu.make_async_copy(late_shard, w_late.at[lax.axis_index("dp")], local.at[7])
    own_late.start()

    share = route_weights[...] / jnp.sum(route_weights[...], axis=0, keepdims=True)
    high = share.astype(BF16).astype(F32)
    low = share - high
    at_row = lax.broadcasted_iota(jnp.int32, (EXTRA, TOK), 0)
    table = jnp.zeros((EXTRA, TOK), F32)
    for k in range(routes.shape[0]):
        named = routes[k : k + 1]
        table += jnp.where(at_row == named, high[k : k + 1], 0.0)
        table += jnp.where(at_row == named + 16, low[k : k + 1], 0.0)
    moe_in[:, D:] = table.T.astype(BF16)

    gather.rest(
        [
            early.steps((0, 1)),
            early.steps((1, 1), (0, 2)),
            early.steps((1, 2)),
            early.steps((0, 3), (1, 3), then=late.start),
            early.steps((0, 4), (1, 4)),
            late.steps((0, 1)),
        ]
    )
    early.finish()
    share_out.start()
    owns = []
    for half, (f, s, _) in enumerate(spots):
        source = w_all.at[pl.ds(8 * half, 8), pl.ds(512, 256)]
        owns.append(pltpu.make_async_copy(source, wo.at[half, :, s], local.at[5 + half]))
        owns[-1].start()

    def rope(part, rows):
        return part * cosine[rows] + pltpu.roll(part, HD // 2, 1) * sine[rows]

    def project(i):
        rows = slice(i * 256, i * 256 + 256)
        left = x[i * 4 : i * 4 + 4].reshape(256, D)
        q = jnp.dot(left, w_all[:, 0:256].reshape(D, 256), preferred_element_type=F32)
        for head in (0, 1):
            queries[head, rows] = rope(q[:, head * HD : (head + 1) * HD], rows).astype(BF16)
        kv = jnp.dot(left, w_all[:, 256:512].reshape(D, 256), preferred_element_type=F32)
        keys[rows] = rope(kv[:, :HD], rows).astype(BF16)
        values[rows] = kv[:, HD:].astype(BF16)

    def attention(i):
        many = (i + 1) * 256
        for head in (0, 1):
            scores = lax.dot_general(
                queries[head, i * 256 : many], keys[0:many], (((1,), (1,)), ((), ())), preferred_element_type=F32
            ) * (1.0 / math.sqrt(HD))
            at_row = lax.broadcasted_iota(jnp.int32, (256, many), 0) + i * 256
            at_col = lax.broadcasted_iota(jnp.int32, (256, many), 1)
            scores = jnp.where(at_row >= at_col, scores, -1e30)
            grown = jnp.exp(scores - jnp.max(scores, axis=-1, keepdims=True))
            total = jnp.sum(grown, axis=-1, keepdims=True)
            part = jnp.dot(grown.astype(BF16), values[0:many], preferred_element_type=F32) / total
            mixed[i, :, :, head * HD : (head + 1) * HD] = part.astype(BF16).reshape(4, TOK, HD)

    for i in range(4):
        project(i)
    share_out.forward()
    late.steps((1, 1), (2, 1))()
    for i in range(4):
        attention(i)

    def rows_of(half, second):
        return mixed.at[second] if half else mixed.at[:, second]

    swaps = []
    for i, step in enumerate((1, 3, 2)):
        for half, (f, s, device) in enumerate(spots):
            cols = pl.ds(pl.multiple_of(s * 256, 256), 256)
            to = turn(s, step)
            swaps.append(
                remote(rows_of(half, to), mx.at[half, :, :, cols], mx_sends, mx_recvs, half * 3 + i, device(f, to))
            )
    keeps = []
    for half, (f, s, device) in enumerate(spots):
        cols = pl.ds(pl.multiple_of(s * 256, 256), 256)
        keeps.append(pltpu.make_async_copy(rows_of(half, s), mx.at[half, :, :, cols], local.at[half]))
        keeps[-1].start()
    share_out.finish()
    late.steps((3, 1), (0, 2))()
    for copy in keeps + owns:
        copy.wait()
    for copy in swaps:
        copy.wait_recv()
    share_out.arrive()

    fold = Fold(spots, y, small, large, None, sends, recvs, HALF)
    for half in (0, 1):
        left = mx[half].reshape(256, 1024)
        for c in range(8):
            part = jnp.dot(left, wo[half, c].reshape(1024, 256), preferred_element_type=F32)
            y[half, :, :, c * 256 : c * 256 + 256] = part.astype(BF16).reshape(4, TOK, 256)
        fold.start(0, (half,))
    for copy in swaps:
        copy.wait_send()
    share_out.drain()
    late.steps((1, 2), (2, 2))()
    fold.middle(0)
    for half in (0, 1):
        cols = slice(half * 2048, (half + 1) * 2048)
        residual[:, cols] = tokens[:, cols].astype(F32) + fold.total(half)
    moe_in[:, 0:D] = normalized(residual[...], moe_gain[...]).astype(BF16)

    def late_block(r, half, second, start, rows):
        return everyone.at[r, half, second, pl.ds(start, rows)]

    gather = Gather(spots, late_block, out_sends, out_recvs, lambda half: moe_in.at[pl.ds(half * HALF, HALF)], False)
    gather.first_hop()
    keeps = []
    for half, (_, s, _) in enumerate(spots):
        keeps.append(pltpu.make_async_copy(gather.own(half), late_block(0, half, s, 0, HALF), local.at[half]))
        keeps[-1].start()
    fold.drain()
    late.steps((3, 2), (0, 3))()
    gather.rest(
        [
            late.steps((1, 3)),
            late.steps((2, 3)),
            late.steps((3, 3), (0, 4)),
            late.steps((1, 4), (2, 4)),
            late.steps((3, 4)),
            late.steps(),
        ]
    )
    for keep in keeps:
        keep.wait()
    late.finish()
    own_late.wait()


def experts(
    everyone, weights, residual,
    out,
    g, w, wd, act, y, small, large, z, sends, recvs, load_g, load_w, load_down,
):
    spots = place()
    rows_of = [pltpu.make_async_copy(everyone.at[r], g.at[r], load_g.at[r]) for r in range(4)]
    feeds = []
    for c in range(6):
        part = (c // 2 + c % 2 * 3) * 256
        view = pl.ds(part, 256)
        feeds.append(pltpu.make_async_copy(weights.at[:, view], w.at[:, view], load_w.at[c]))
    downs = pltpu.make_async_copy(weights.at[:, pl.ds(2 * FF, FF)], wd, load_down)
    rows_of[3].start()
    for copy in feeds:
        copy.start()
    downs.start()
    for r in (2, 1, 0):
        rows_of[r].start()
    meet(around(spots))
    scatter = Scatter(spots, y, small, large, z, sends, recvs)
    index = lax.axis_index("expert")

    def feed_part(r, c):
        cols = pl.ds(c * 256, 256)
        left = g[r, :, :, :, 0:D].reshape(256, D)
        gate = jnp.dot(left, w[:, cols].reshape(D, 256), preferred_element_type=F32)
        up = jnp.dot(left, w[:, pl.ds(FF + c * 256, 256)].reshape(D, 256), preferred_element_type=F32)
        act[:, cols] = (gate / (1.0 + jnp.exp(-gate)) * up).astype(BF16)

    def feed(r):
        rows_of[r].wait()
        for c in range(3):
            if r == 3:
                feeds[2 * c].wait()
                feeds[2 * c + 1].wait()
            feed_part(r, c)

    def down(r):
        table = g[r, :, :, :, D:].reshape(256, EXTRA).astype(F32)
        lanes = lax.broadcasted_iota(jnp.int32, (256, EXTRA), 1)
        chosen = (lanes == index) | (lanes == index + 16)
        share = jnp.sum(jnp.where(chosen, table, 0.0), axis=-1, keepdims=True)

        for n in range(16):
            right = wd[:, n * 48 : n * 48 + 48].reshape(FF, 256)
            part = jnp.dot(act[...], right, preferred_element_type=F32) * share
            y[r, :, :, :, n * 256 : n * 256 + 256] = part.astype(BF16).reshape(2, 4, HALF, 256)

    feed(3)
    downs.wait()
    down(3)
    scatter.start(3)
    feed(2)
    scatter.middle(3)
    down(2)
    scatter.start(2)
    feed(1)
    scatter.middle(2)
    scatter.finish(3)
    scatter.start(4)
    down(1)
    scatter.start(1)
    feed(0)
    scatter.middle(1)
    scatter.finish(2)
    down(0)
    scatter.start(0)
    scatter.finish(1)
    scatter.middle(4)
    scatter.middle(0)
    scatter.finish(0)
    for half in (0, 1):
        rows = slice(half * HALF, (half + 1) * HALF)
        out[rows] = (residual[rows] + scatter.total(half)).astype(BF16)
    scatter.drain()


def rope_tables():
    frequency = np.exp(np.arange(HD // 2, dtype=np.float32) * np.float32(-2.0 * math.log(1000000.0) / HD))
    angles = (np.arange(SEQ, dtype=np.float32)[:, None] * frequency[None, :]).astype(np.float32)
    cosine, sine = np.cos(angles), np.sin(angles)
    return (
        np.concatenate([cosine, cosine], axis=1).astype(np.float32),
        np.concatenate([-sine, sine], axis=1).astype(np.float32),
    )


VMEM = pl.BlockSpec(memory_space=pltpu.VMEM)
ANY = pl.BlockSpec(memory_space=pl.ANY)
HBM = pl.BlockSpec(memory_space=pltpu.HBM)
SEMS = pltpu.SemaphoreType.DMA((40,))
RING = [
    pltpu.VMEM((4, 2, 4, HALF, D), BF16),
    pltpu.VMEM((2, 5, 2, 16, D), BF16),
    pltpu.VMEM((2, 5, 2, HALF, D), BF16),
    pltpu.VMEM((2, 4, HALF, D), BF16),
]


def params(number, mib):
    return pltpu.CompilerParams(collective_id=number, has_side_effects=True, vmem_limit_bytes=mib * MIB)


def cost(flops, moved):
    return pl.CostEstimate(flops=flops, bytes_accessed=moved, transcendentals=0)


def local(
    tokens,
    attn_gain,
    moe_gain,
    w_query,
    w_key,
    w_value,
    w_out,
    expert_gate,
    expert_up,
    expert_down,
    routes,
    route_weights,
):
    rows = tokens[0]
    cosine, sine = rope_tables()
    residual, everyone, w_late = pl.pallas_call(
        attend,
        out_shape=(
            jax.ShapeDtypeStruct((TOK, D), F32),
            jax.ShapeDtypeStruct((4, 2, 4, HALF, D + EXTRA), BF16),
            jax.ShapeDtypeStruct((16, 2304, 256), BF16),
        ),
        in_specs=[VMEM] * 7 + [ANY] * 7,
        out_specs=(VMEM, HBM, HBM),
        scratch_shapes=[
            pltpu.VMEM((TOK, D), BF16),
            pltpu.VMEM((4, 256, 256), BF16),
            pltpu.VMEM((2, 256, FF), BF16),
            pltpu.VMEM((48, D), BF16),
            pltpu.VMEM((768, 256), BF16),
            pltpu.VMEM((2304, 256), BF16),
            pltpu.VMEM((16, TOK, D), BF16),
            pltpu.VMEM((16, 768, 256), BF16),
            pltpu.VMEM((2, 8, 4, 256, 256), BF16),
            pltpu.VMEM((2, SEQ, HD), BF16),
            pltpu.VMEM((SEQ, HD), BF16),
            pltpu.VMEM((SEQ, HD), BF16),
            pltpu.VMEM((4, 4, TOK, 256), BF16),
            pltpu.VMEM((2, 4, TOK, 1024), BF16),
            pltpu.VMEM((TOK, D + EXTRA), BF16),
            pltpu.VMEM((2, 4, TOK, 2048), BF16),
            pltpu.VMEM((2, 1, 2, HALF, 2048), BF16),
            pltpu.VMEM((2, 1, 2, TOK, 2048), BF16),
            SEMS,
            SEMS,
            pltpu.SemaphoreType.DMA((2, 17)),
            pltpu.SemaphoreType.DMA((2, 17)),
            pltpu.SemaphoreType.DMA((16,)),
            pltpu.SemaphoreType.DMA((16,)),
            pltpu.SemaphoreType.DMA((6,)),
            pltpu.SemaphoreType.DMA((6,)),
            SEMS,
            SEMS,
            SEMS,
            SEMS,
            pltpu.SemaphoreType.DMA((4, 17)),
            pltpu.SemaphoreType.DMA((4, 17)),
            pltpu.SemaphoreType.DMA((8,)),
        ],
        compiler_params=params(1, 60),
        cost_estimate=cost(8 << 30, 64 * MIB),
        name="attention",
    )(
        rows, attn_gain[None], moe_gain[None], routes[0].T, route_weights[0].T, cosine, sine,
        expert_gate[0], expert_up[0], expert_down[0], w_query, w_key, w_value, w_out,
    )

    layer_out = pl.pallas_call(
        experts,
        out_shape=jax.ShapeDtypeStruct((TOK, D), BF16),
        in_specs=[ANY, ANY, VMEM],
        out_specs=VMEM,
        scratch_shapes=[
            pltpu.VMEM((4, 2, 4, HALF, D + EXTRA), BF16),
            pltpu.VMEM((16, 1536, 256), BF16),
            pltpu.VMEM((16, 768, 256), BF16),
            pltpu.VMEM((256, FF), BF16),
            *RING,
            SEMS,
            SEMS,
            pltpu.SemaphoreType.DMA((4,)),
            pltpu.SemaphoreType.DMA((6,)),
            pltpu.SemaphoreType.DMA,
        ],
        compiler_params=params(2, 60),
        cost_estimate=cost(20 << 30, 200 * MIB),
        name="experts",
    )(everyone, w_late, residual)
    return layer_out[None]


def solution(mesh):
    return jax.shard_map(
        local,
        mesh=mesh,
        in_specs=(
            P("dp", "expert", None),
            P(),
            P(),
            P("dp", "expert"),
            P("dp", None),
            P("dp", None),
            P("expert", "dp"),
            P("expert", "dp", None),
            P("expert", "dp", None),
            P("expert", "dp", None),
            P("dp", "expert", None),
            P("dp", "expert", None),
        ),
        out_specs=P("dp", "expert", None),
        check_vma=False,
    )
```

```python
import functools
import math

import jax
import jax.numpy as jnp
import numpy as np
from jax import lax
from jax.experimental import pallas as pl
from jax.experimental.pallas import tpu as pltpu
from jax.sharding import PartitionSpec as P

HD = 128
D = 4096
FF = 768
TOK = 64
HALF = 32
SEQ = 1024
EXTRA = 128
EARLY = ((0, 512), (512, 256))
LATE = ((0, 576), (576, 576), (1152, 576), (1728, 576))
MESH = pl.DeviceIdType.MESH
F32 = jnp.float32
BF16 = jnp.bfloat16
MIB = 1 << 20

STEP = (0, 3, 1, 2)


def place():
    index = lax.axis_index("expert")
    x, y = index // 4, index % 4
    return (
        (x, y, lambda first, second: {"expert": first * 4 + second}),
        (y, x, lambda first, second: {"expert": second * 4 + first}),
    )


def turn(coordinate, step):
    return (coordinate + step) % 4


def around(spots):
    return [device(turn(f, step), s) for f, s, device in spots for step in (1, 3)]


def meet(devices):
    barrier = pltpu.get_barrier_semaphore()
    for device in devices:
        pl.semaphore_signal(barrier, inc=1, device_id=device, device_id_type=MESH)
    pl.semaphore_wait(barrier, len(devices))


def remote(source, target, sends, recvs, slot, device):
    copy = pltpu.make_async_remote_copy(
        src_ref=source,
        dst_ref=target,
        send_sem=sends.at[slot],
        recv_sem=recvs.at[slot],
        device_id=device,
        device_id_type=MESH,
    )
    copy.start()
    return copy


class Gather:
    def __init__(self, spots, block, sends, recvs, own, absolute):
        self.spots, self.block, self.sends, self.recvs = spots, block, sends, recvs
        self.own, self.absolute = own, absolute
        self.copies = {}

    def send(self, half, group, lane, source, target, device):
        slot = (half * 5 + group) * 4 + lane
        self.copies[half, group, lane] = remote(
            source, target, self.sends, self.recvs, slot, device
        )

    def first_hop(self):
        for half, (f, s, device) in enumerate(self.spots):
            for lane, step in ((0, 1), (1, 3)):
                target = self.block(0 if self.absolute else 1 + lane, half, s, 0, HALF)
                self.send(half, 4, lane, self.own(half), target, device(turn(f, step), s))
        self.spread(0)

    def spread(self, r, halves=(0, 1)):
        for half in halves:
            f, s, device = self.spots[half]
            mine = self.own(half) if r == 0 else self.block(r, half, s, 0, HALF)
            for lane, step in ((0, 1), (1, 3)):
                self.send(half, r, lane, mine, self.block(r, half, s, 0, HALF), device(f, turn(s, step)))

    def second_hop(self):
        for lane, step in ((0, 1), (1, 3)):
            for half, (f, s, device) in enumerate(self.spots):
                self.copies[half, 4, lane].wait_recv()
                source = self.block(1 + lane, half, s, lane * 16, 16)
                target = source if self.absolute else self.block(3, half, s, lane * 16, 16)
                self.send(half, 4, 2 + lane, source, target, device(turn(f, step), s))

    def last_hop(self):
        for half in (0, 1):
            for lane in (2, 3):
                self.copies[half, 4, lane].wait_recv()
            self.spread(3, (half,))

    def forward(self, r):
        for lane, step in ((0, 1), (1, 3)):
            for half, (f, s, device) in enumerate(self.spots):
                self.copies[half, r, lane].wait_recv()
                here = self.block(r, half, turn(s, 4 - step), lane * 16, 16)
                self.send(half, r, 2 + lane, here, here, device(f, turn(s, step)))

    def finish(self, r):
        for half in (0, 1):
            for lane in (2, 3):
                self.copies[half, r, lane].wait_recv()

    def rest(self, between):
        self.second_hop()
        self.forward(0)
        between[0]()
        self.spread(1)
        self.last_hop()
        self.spread(2)
        between[1]()
        self.forward(1)
        between[2]()
        self.forward(3)
        between[3]()
        self.forward(2)
        between[4]()
        for r in range(4):
            self.finish(r)
        between[5]()
        self.drain()

    def drain(self):
        for copy in self.copies.values():
            copy.wait_send()


class Scatter:
    def __init__(self, spots, y_ref, small, large, z_ref, sends, recvs, cut=HALF // 2):
        self.spots, self.y, self.small, self.large, self.z = spots, y_ref, small, large, z_ref
        self.sends, self.recvs, self.cut = sends, recvs, cut
        self.copies = {}

    def send(self, half, group, lane, source, target, device):
        slot = (half * 5 + group) * 4 + lane
        self.copies[half, group, lane] = remote(
            source, target, self.sends, self.recvs, slot, device
        )

    def parts(self, half, group):
        f, s, device = self.spots[half]
        if group < 4:
            return (
                lambda step: self.y.at[group, half, turn(s, step)],
                lambda step: device(f, turn(s, step)),
            )
        return (
            lambda step: self.z.at[half, STEP.index(step)],
            lambda step: device(turn(f, step), s),
        )

    def start(self, group, halves=(0, 1)):
        for half in halves:
            block, device = self.parts(half, group)
            for lane, step in ((0, 1), (1, 3)):
                self.send(
                    half, group, lane, block(2).at[pl.ds(lane * self.cut, self.cut)], self.small.at[half, group, lane],
                    device(step),
                )

    def middle(self, group):
        for lane, step in ((0, 1), (1, 3)):
            for half in (0, 1):
                block, device = self.parts(half, group)
                self.copies[half, group, lane].wait_recv()
                rows = block(step).at[pl.ds(lane * self.cut, self.cut)]
                rows[...] = (rows[...].astype(F32) + self.small[half, group, lane].astype(F32)).astype(BF16)
                self.send(half, group, 2 + lane, block(step), self.large.at[half, group, lane], device(step))

    def arrived(self, half, group):
        for lane in (2, 3):
            self.copies[half, group, lane].wait_recv()
        return self.large[half, group, 0].astype(F32) + self.large[half, group, 1].astype(F32)

    def finish(self, group):
        for half in (0, 1):
            _, s, _ = self.spots[half]
            total = self.arrived(half, group) + self.y[group, half, s].astype(F32)
            self.z[half, group] = total.astype(BF16)

    def total(self, half):
        return self.arrived(half, 4) + self.z[half, 0].astype(F32)

    def drain(self):
        for copy in self.copies.values():
            copy.wait_send()


class Fold(Scatter):
    def parts(self, half, group):
        f, s, device = self.spots[half]
        return (lambda step: self.y.at[half, turn(f, step)], lambda step: device(turn(f, step), s))

    def total(self, half):
        return self.arrived(half, 0) + self.y[half, self.spots[half][0]].astype(F32)


class Column:
    def __init__(self, mine, w_ref, base, rows, sends, recvs):
        index = lax.axis_index("dp")
        self.mine, self.w, self.base, self.rows, self.sends, self.recvs = mine, w_ref, base, rows, sends, recvs
        self.level, self.core = index // 2, index % 2
        self.other = {"dp": self.level * 2 + 1 - self.core}
        self.next = [{"dp": (self.level + step) % 8 * 2 + self.core} for step in (1, 7)]
        self.copies = {}

    def send(self, slot, step, device, way=None):
        start, rows = (0, self.rows) if way is None else (way * self.rows // 2, self.rows // 2)
        place = self.w.at[(self.level + step) % 8 * 2 + self.core, pl.ds(self.base + start, rows)]
        source = place if step else self.mine
        self.copies[slot] = remote(source, place, self.sends, self.recvs, slot, device)

    def start(self):
        for way in (0, 1):
            self.send(way * 4, 0, self.next[way])
        self.send(8, 0, self.other)

    def step(self, t):
        for way in (0, 1):
            self.copies[way * 4 + t - 1].wait_recv()
            here = t if way else 8 - t
            if t < 4:
                self.send(way * 4 + t, here, self.next[way], way if t == 3 else None)
            self.send(8 + way * 4 + t, here, self.other, way if t == 4 else None)

    def finish(self):
        for slot in range(8, 17):
            self.copies[slot].wait_recv()
        for copy in self.copies.values():
            copy.wait_send()


class Columns:
    def __init__(self, mine, w_ref, parts, sends, recvs):
        self.all = [
            Column(mine.at[pl.ds(base, rows)], w_ref, base, rows, sends.at[i], recvs.at[i])
            for i, (base, rows) in enumerate(parts)
        ]
        self.near = self.all[0].next + [self.all[0].other]

    def start(self, parts=None):
        for which in range(len(self.all)) if parts is None else parts:
            self.all[which].start()

    def steps(self, *todo, then=None):
        def run():
            for which, t in todo:
                self.all[which].step(t)
            if then:
                then()

        return run

    def finish(self):
        for column in self.all:
            column.finish()


def normalized(values, gain):
    return values * lax.rsqrt(jnp.mean(values * values, axis=-1, keepdims=True) + 1e-06) * gain


class Share:
    def __init__(self, spots, weights, wo, sends, recvs):
        index = lax.axis_index("dp")
        self.core = index % 2
        self.other = {"dp": index + 1 - 2 * self.core}
        self.spots, self.weights, self.wo, self.sends, self.recvs = spots, weights, wo, sends, recvs
        self.copies = {}

    def block(self, half, second, start, count):
        return self.wo.at[half, pl.ds(4 * self.core + start, count), second]

    def send(self, half, lane, source, target, device):
        self.copies[half, lane] = remote(source, target, self.sends, self.recvs, half * 8 + lane, device)

    def start(self):
        for half, (f, s, device) in enumerate(self.spots):
            source = self.weights.at[pl.ds(8 * half + 4 * self.core, 4), pl.ds(512, 256)]
            for lane, step in ((0, 1), (1, 3)):
                self.send(half, lane, source, self.block(half, s, 0, 4), device(f, turn(s, step)))

    def forward(self):
        for lane, step in ((0, 1), (1, 3)):
            for half, (f, s, device) in enumerate(self.spots):
                self.copies[half, lane].wait_recv()
                here = self.block(half, turn(s, 4 - step), 2 * lane, 2)
                self.send(half, 2 + lane, here, here, device(f, turn(s, step)))
                here = self.block(half, turn(s, 4 - step), 0, 4)
                self.send(half, 4 + lane, here, here, self.other)

    def finish(self):
        for lane in (0, 1):
            for half, (f, s, device) in enumerate(self.spots):
                self.copies[half, 2 + lane].wait_recv()
                here = self.block(half, turn(s, 2), 2 * lane, 2)
                self.send(half, 6 + lane, here, here, self.other)

    def arrive(self):
        for half in (0, 1):
            for lane in range(4, 8):
                self.copies[half, lane].wait_recv()

    def drain(self):
        for copy in self.copies.values():
            copy.wait_send()


def attend(
    tokens, attn_gain, moe_gain, routes, route_weights, cosine, sine,
    gate, up, down, w_query, w_key, w_value, w_out,
    residual, everyone, w_late,
    own, parts, wide, tall, shard, late_shard, x, w_all, wo, queries, keys, values, mixed, mx, moe_in, y, small, large,
    in_sends, in_recvs, w_sends, w_recvs, wo_sends, wo_recvs, mx_sends, mx_recvs, sends, recvs, out_sends, out_recvs,
    z_sends, z_recvs, local,
):
    spots = place()
    index = lax.axis_index("expert")
    loads = [
        pltpu.make_async_copy(source, target, local.at[i])
        for i, (source, target) in enumerate(
            (
                (w_query, parts.at[0]),
                (w_key, parts.at[1]),
                (w_value, parts.at[2]),
                (w_out, parts.at[3]),
                (down, tall),
                (gate, wide.at[0]),
                (up, wide.at[1]),
            )
        )
    ]
    for copy in loads:
        copy.start()
    own[...] = normalized(tokens[...].astype(F32), attn_gain[...]).astype(BF16)
    x[index] = own[...]
    early = Columns(shard, w_all, EARLY, w_sends, w_recvs)
    late = Columns(late_shard, w_late, LATE, z_sends, z_recvs)
    share_out = Share(spots, w_all, wo, wo_sends, wo_recvs)
    across = [device(f, turn(s, 2)) for f, s, device in spots]
    meet(around(spots) + across + early.near)

    def block(r, half, second, start, rows):
        f, _, device = spots[half]
        return x.at[device(turn(f, STEP[r]), second)["expert"], pl.ds(half * HALF + start, rows)]

    gather = Gather(spots, block, in_sends, in_recvs, lambda half: own.at[pl.ds(half * HALF, HALF)], True)
    gather.first_hop()

    for copy in loads:
        copy.wait()
    key_cols = pl.ds(pl.multiple_of(index // 8 * HD, HD), HD)
    shard[0:256] = parts[0]
    shard[256:512, 0:HD] = parts[1, :, key_cols]
    shard[256:512, HD:] = parts[2, :, key_cols]
    shard[512:768] = parts[3]
    w_all[lax.axis_index("dp")] = shard[...]
    early.start()
    for c in range(6):
        late_shard[c * 256 : c * 256 + 256] = wide[c // 3, :, c % 3 * 256 : c % 3 * 256 + 256]
    for c in range(16):
        late_shard[2 * FF + c * 48 : 2 * FF + c * 48 + 48] = tall[:, c * 256 : c * 256 + 256]

    own_late = pltpu.make_async_copy(late_shard, w_late.at[lax.axis_index("dp")], local.at[7])
    own_late.start()

    share = route_weights[...] / jnp.sum(route_weights[...], axis=0, keepdims=True)
    high = share.astype(BF16).astype(F32)
    low = share - high
    at_row = lax.broadcasted_iota(jnp.int32, (EXTRA, TOK), 0)
    table = jnp.zeros((EXTRA, TOK), F32)
    for k in range(routes.shape[0]):
        named = routes[k : k + 1]
        table += jnp.where(at_row == named, high[k : k + 1], 0.0)
        table += jnp.where(at_row == named + 16, low[k : k + 1], 0.0)
    moe_in[:, D:] = table.T.astype(BF16)

    owns = []

    def begin_share():
        early.finish()
        share_out.start()
        for half, (f, s, _) in enumerate(spots):
            source = w_all.at[pl.ds(8 * half, 8), pl.ds(512, 256)]
            owns.append(pltpu.make_async_copy(source, wo.at[half, :, s], local.at[5 + half]))
            owns[-1].start()

    gather.rest(
        [
            early.steps((0, 1)),
            early.steps((1, 1), (0, 2)),
            early.steps((1, 2), then=lambda: late.start((0,))),
            early.steps((0, 3), (1, 3), then=lambda: late.start((1, 2, 3))),
            early.steps((0, 4), (1, 4), then=begin_share),
            late.steps((0, 1)),
        ]
    )
    def rope(part, rows):
        return part * cosine[rows] + pltpu.roll(part, HD // 2, 1) * sine[rows]

    def project(i):
        rows = slice(i * 256, i * 256 + 256)
        left = x[i * 4 : i * 4 + 4].reshape(256, D)
        q = jnp.dot(left, w_all[:, 0:256].reshape(D, 256), preferred_element_type=F32)
        for head in (0, 1):
            queries[head, rows] = rope(q[:, head * HD : (head + 1) * HD], rows).astype(BF16)
        kv = jnp.dot(left, w_all[:, 256:512].reshape(D, 256), preferred_element_type=F32)
        keys[rows] = rope(kv[:, :HD], rows).astype(BF16)
        values[rows] = kv[:, HD:].astype(BF16)

    def attention(i):
        many = (i + 1) * 256
        for head in (0, 1):
            scores = lax.dot_general(
                queries[head, i * 256 : many], keys[0:many], (((1,), (1,)), ((), ())), preferred_element_type=F32
            ) * (1.0 / math.sqrt(HD))
            at_row = lax.broadcasted_iota(jnp.int32, (256, many), 0) + i * 256
            at_col = lax.broadcasted_iota(jnp.int32, (256, many), 1)
            scores = jnp.where(at_row >= at_col, scores, -1e30)
            grown = jnp.exp(scores - jnp.max(scores, axis=-1, keepdims=True))
            total = jnp.sum(grown, axis=-1, keepdims=True)
            part = jnp.dot(grown.astype(BF16), values[0:many], preferred_element_type=F32) / total
            mixed[i, :, :, head * HD : (head + 1) * HD] = part.astype(BF16).reshape(4, TOK, HD)

    for i in range(4):
        project(i)
    share_out.forward()
    late.steps((1, 1), (2, 1))()
    for i in range(4):
        attention(i)

    def rows_of(half, second):
        return mixed.at[second] if half else mixed.at[:, second]

    swaps = []
    for i, step in enumerate((1, 3, 2)):
        for half, (f, s, device) in enumerate(spots):
            cols = pl.ds(pl.multiple_of(s * 256, 256), 256)
            to = turn(s, step)
            swaps.append(
                remote(rows_of(half, to), mx.at[half, :, :, cols], mx_sends, mx_recvs, half * 3 + i, device(f, to))
            )
    keeps = []
    for half, (f, s, device) in enumerate(spots):
        cols = pl.ds(pl.multiple_of(s * 256, 256), 256)
        keeps.append(pltpu.make_async_copy(rows_of(half, s), mx.at[half, :, :, cols], local.at[half]))
        keeps[-1].start()
    share_out.finish()
    late.steps((3, 1), (0, 2))()
    for copy in keeps + owns:
        copy.wait()
    for copy in swaps:
        copy.wait_recv()
    share_out.arrive()

    fold = Fold(spots, y, small, large, None, sends, recvs, HALF)
    for half in (0, 1):
        left = mx[half].reshape(256, 1024)
        for c in range(8):
            part = jnp.dot(left, wo[half, c].reshape(1024, 256), preferred_element_type=F32)
            y[half, :, :, c * 256 : c * 256 + 256] = part.astype(BF16).reshape(4, TOK, 256)
        fold.start(0, (half,))
    for copy in swaps:
        copy.wait_send()
    share_out.drain()
    late.steps((1, 2), (2, 2))()
    fold.middle(0)
    for half in (0, 1):
        cols = slice(half * 2048, (half + 1) * 2048)
        residual[:, cols] = tokens[:, cols].astype(F32) + fold.total(half)
    moe_in[:, 0:D] = normalized(residual[...], moe_gain[...]).astype(BF16)

    def late_block(r, half, second, start, rows):
        return everyone.at[r, half, second, pl.ds(start, rows)]

    gather = Gather(spots, late_block, out_sends, out_recvs, lambda half: moe_in.at[pl.ds(half * HALF, HALF)], False)
    gather.first_hop()
    keeps = []
    for half, (_, s, _) in enumerate(spots):
        keeps.append(pltpu.make_async_copy(gather.own(half), late_block(0, half, s, 0, HALF), local.at[half]))
        keeps[-1].start()
    fold.drain()
    late.steps((3, 2), (0, 3))()
    gather.rest(
        [
            late.steps((1, 3)),
            late.steps((2, 3)),
            late.steps((3, 3), (0, 4)),
            late.steps((1, 4), (2, 4)),
            late.steps((3, 4)),
            late.steps(),
        ]
    )
    for keep in keeps:
        keep.wait()
    late.finish()
    own_late.wait()


def experts(
    everyone, weights, residual,
    out,
    g, w, wd, act, y, small, large, z, sends, recvs, load_g, load_w, load_down,
):
    spots = place()
    rows_of = [pltpu.make_async_copy(everyone.at[r], g.at[r], load_g.at[r]) for r in range(4)]
    feeds = []
    for c in range(6):
        part = (c // 2 + c % 2 * 3) * 256
        view = pl.ds(part, 256)
        feeds.append(pltpu.make_async_copy(weights.at[:, view], w.at[:, view], load_w.at[c]))
    downs = pltpu.make_async_copy(weights.at[:, pl.ds(2 * FF, FF)], wd, load_down)
    rows_of[3].start()
    for copy in feeds:
        copy.start()
    downs.start()
    for r in (2, 1, 0):
        rows_of[r].start()
    meet(around(spots))
    scatter = Scatter(spots, y, small, large, z, sends, recvs)
    index = lax.axis_index("expert")

    def feed_part(r, c):
        cols = pl.ds(c * 256, 256)
        left = g[r, :, :, :, 0:D].reshape(256, D)
        gate = jnp.dot(left, w[:, cols].reshape(D, 256), preferred_element_type=F32)
        up = jnp.dot(left, w[:, pl.ds(FF + c * 256, 256)].reshape(D, 256), preferred_element_type=F32)
        act[:, cols] = (gate / (1.0 + jnp.exp(-gate)) * up).astype(BF16)

    def feed(r):
        rows_of[r].wait()
        for c in range(3):
            if r == 3:
                feeds[2 * c].wait()
                feeds[2 * c + 1].wait()
            feed_part(r, c)

    def down(r):
        table = g[r, :, :, :, D:].reshape(256, EXTRA).astype(F32)
        lanes = lax.broadcasted_iota(jnp.int32, (256, EXTRA), 1)
        chosen = (lanes == index) | (lanes == index + 16)
        share = jnp.sum(jnp.where(chosen, table, 0.0), axis=-1, keepdims=True)

        for n in range(16):
            right = wd[:, n * 48 : n * 48 + 48].reshape(FF, 256)
            part = jnp.dot(act[...], right, preferred_element_type=F32) * share
            y[r, :, :, :, n * 256 : n * 256 + 256] = part.astype(BF16).reshape(2, 4, HALF, 256)

    feed(3)
    downs.wait()
    down(3)
    scatter.start(3)
    feed(2)
    scatter.middle(3)
    down(2)
    scatter.start(2)
    feed(1)
    scatter.middle(2)
    scatter.finish(3)
    scatter.start(4)
    down(1)
    scatter.start(1)
    feed(0)
    scatter.middle(1)
    scatter.finish(2)
    down(0)
    scatter.start(0)
    scatter.finish(1)
    scatter.middle(4)
    scatter.middle(0)
    scatter.finish(0)
    for half in (0, 1):
        rows = slice(half * HALF, (half + 1) * HALF)
        out[rows] = (residual[rows] + scatter.total(half)).astype(BF16)
    scatter.drain()


def rope_tables():
    frequency = np.exp(np.arange(HD // 2, dtype=np.float32) * np.float32(-2.0 * math.log(1000000.0) / HD))
    angles = (np.arange(SEQ, dtype=np.float32)[:, None] * frequency[None, :]).astype(np.float32)
    cosine, sine = np.cos(angles), np.sin(angles)
    return (
        np.concatenate([cosine, cosine], axis=1).astype(np.float32),
        np.concatenate([-sine, sine], axis=1).astype(np.float32),
    )


VMEM = pl.BlockSpec(memory_space=pltpu.VMEM)
ANY = pl.BlockSpec(memory_space=pl.ANY)
HBM = pl.BlockSpec(memory_space=pltpu.HBM)
SEMS = pltpu.SemaphoreType.DMA((40,))
RING = [
    pltpu.VMEM((4, 2, 4, HALF, D), BF16),
    pltpu.VMEM((2, 5, 2, 16, D), BF16),
    pltpu.VMEM((2, 5, 2, HALF, D), BF16),
    pltpu.VMEM((2, 4, HALF, D), BF16),
]


def params(number, mib):
    return pltpu.CompilerParams(collective_id=number, has_side_effects=True, vmem_limit_bytes=mib * MIB)


def cost(flops, moved):
    return pl.CostEstimate(flops=flops, bytes_accessed=moved, transcendentals=0)


def local(
    tokens,
    attn_gain,
    moe_gain,
    w_query,
    w_key,
    w_value,
    w_out,
    expert_gate,
    expert_up,
    expert_down,
    routes,
    route_weights,
):
    rows = tokens[0]
    cosine, sine = rope_tables()
    residual, everyone, w_late = pl.pallas_call(
        attend,
        out_shape=(
            jax.ShapeDtypeStruct((TOK, D), F32),
            jax.ShapeDtypeStruct((4, 2, 4, HALF, D + EXTRA), BF16),
            jax.ShapeDtypeStruct((16, 2304, 256), BF16),
        ),
        in_specs=[VMEM] * 7 + [ANY] * 7,
        out_specs=(VMEM, HBM, HBM),
        scratch_shapes=[
            pltpu.VMEM((TOK, D), BF16),
            pltpu.VMEM((4, 256, 256), BF16),
            pltpu.VMEM((2, 256, FF), BF16),
            pltpu.VMEM((48, D), BF16),
            pltpu.VMEM((768, 256), BF16),
            pltpu.VMEM((2304, 256), BF16),
            pltpu.VMEM((16, TOK, D), BF16),
            pltpu.VMEM((16, 768, 256), BF16),
            pltpu.VMEM((2, 8, 4, 256, 256), BF16),
            pltpu.VMEM((2, SEQ, HD), BF16),
            pltpu.VMEM((SEQ, HD), BF16),
            pltpu.VMEM((SEQ, HD), BF16),
            pltpu.VMEM((4, 4, TOK, 256), BF16),
            pltpu.VMEM((2, 4, TOK, 1024), BF16),
            pltpu.VMEM((TOK, D + EXTRA), BF16),
            pltpu.VMEM((2, 4, TOK, 2048), BF16),
            pltpu.VMEM((2, 1, 2, HALF, 2048), BF16),
            pltpu.VMEM((2, 1, 2, TOK, 2048), BF16),
            SEMS,
            SEMS,
            pltpu.SemaphoreType.DMA((2, 17)),
            pltpu.SemaphoreType.DMA((2, 17)),
            pltpu.SemaphoreType.DMA((16,)),
            pltpu.SemaphoreType.DMA((16,)),
            pltpu.SemaphoreType.DMA((6,)),
            pltpu.SemaphoreType.DMA((6,)),
            SEMS,
            SEMS,
            SEMS,
            SEMS,
            pltpu.SemaphoreType.DMA((4, 17)),
            pltpu.SemaphoreType.DMA((4, 17)),
            pltpu.SemaphoreType.DMA((8,)),
        ],
        compiler_params=params(1, 60),
        cost_estimate=cost(8 << 30, 64 * MIB),
        name="attention",
    )(
        rows, attn_gain[None], moe_gain[None], routes[0].T, route_weights[0].T, cosine, sine,
        expert_gate[0], expert_up[0], expert_down[0], w_query, w_key, w_value, w_out,
    )

    layer_out = pl.pallas_call(
        experts,
        out_shape=jax.ShapeDtypeStruct((TOK, D), BF16),
        in_specs=[ANY, ANY, VMEM],
        out_specs=VMEM,
        scratch_shapes=[
            pltpu.VMEM((4, 2, 4, HALF, D + EXTRA), BF16),
            pltpu.VMEM((16, 1536, 256), BF16),
            pltpu.VMEM((16, 768, 256), BF16),
            pltpu.VMEM((256, FF), BF16),
            *RING,
            SEMS,
            SEMS,
            pltpu.SemaphoreType.DMA((4,)),
            pltpu.SemaphoreType.DMA((6,)),
            pltpu.SemaphoreType.DMA,
        ],
        compiler_params=params(2, 60),
        cost_estimate=cost(20 << 30, 200 * MIB),
        name="experts",
    )(everyone, w_late, residual)
    return layer_out[None]


def solution(mesh):
    return jax.shard_map(
        local,
        mesh=mesh,
        in_specs=(
            P("dp", "expert", None),
            P(),
            P(),
            P("dp", "expert"),
            P("dp", None),
            P("dp", None),
            P("expert", "dp"),
            P("expert", "dp", None),
            P("expert", "dp", None),
            P("expert", "dp", None),
            P("dp", "expert", None),
            P("dp", "expert", None),
        ),
        out_specs=P("dp", "expert", None),
        check_vma=False,
    )
```
